32 devices in a mesh: groups: 2 (over x), cell: 16 (over z, y, core).
Axes of the slice: x: 2, y: 2, z: 4, core: 2. Of those that a mesh axis runs over, the one named last changes fastest.
Arguments:
- positions: float32 [3, 196608], P(None, ('groups', 'cell')), parts along dimension 1, may hold values from -1 to 1
- deltas: float32 [196608], P(('groups', 'cell')), parts along dimension 0, may hold values from 0.02 to 0.1
- background: float32 [3, 2048], P(None, ('groups', 'cell')), parts along dimension 1, may hold values from 0 to 1
- target: float32 [3, 2048], P(None, ('groups', 'cell')), parts along dimension 1, may hold values from 0 to 1
- ray_codes: int32 [2048], P(('groups', 'cell')), parts along dimension 0, may hold values from 0 to 2047
- frequencies: float32 [3, 64], replicated, may hold values from -16 to 16
- w_first: bfloat16 [32, 128, 256], P('cell'), may hold values from -0.5 to 0.5
- b_first: float32 [32, 256], P('cell'), may hold values from -3 to 3
- w_second: bfloat16 [32, 256, 256], P('cell'), may hold values from -0.375 to 0.375
- b_second: float32 [32, 256], P('cell'), may hold values from -3 to 3
- head_out: bfloat16 [32, 4, 256], P('cell'), may hold values from -0.375 to 0.375
- head_app: bfloat16 [32, 3, 48], P('cell'), may hold values from -0.875 to 0.875
- app_table: float32 [48, 2048], replicated, may hold values from -5 to 5
- dispatch: int32 [1024, 192], P(('groups', 'cell')), parts along dimension 0, may hold values from 0 to 6143, as said below
- counts: int32 [1024], P(('groups', 'cell')), parts along dimension 0, may hold values from 0 to 192, as said below
Outputs:
- grad_w_first: float32 [64, 128, 256], P(('groups', 'cell')), parts along dimension 0
- grad_b_first: float32 [64, 256], P(('groups', 'cell')), parts along dimension 0
- grad_w_second: float32 [64, 256, 256], P(('groups', 'cell')), parts along dimension 0
- grad_b_second: float32 [64, 256], P(('groups', 'cell')), parts along dimension 0
- grad_head_out: float32 [64, 4, 256], P(('groups', 'cell')), parts along dimension 0
- grad_head_app: float32 [64, 3, 48], P(('groups', 'cell')), parts along dimension 0
- grad_table: float32 [96, 2048], P('groups'), parts along dimension 0
The draws below stay inside these ranges and needn't reach their ends.
There are 2 independent parts, one for each index of `groups`. The reference program is written for one: setup_inputs(seed, part) draws one part's arguments, and reference() takes and returns one part's arrays. A program takes and returns all parts, laid end to end along the dimension named above; an argument that names none is the same for every part. Nothing has to cross between parts.
Inputs may be any that keep to these rules, and one draw needn't show every extreme that they name: `dispatch`: on each device the 32 x 192 entries are a permutation of its rows 0 to 6143; a row lies in cell c when it stands among the first counts entries of c's list, and in no cell otherwise. `counts`: one cell has 192 samples on every device.
All inputs are finite; a program needn't handle non-finite values.
Results may differ from the reference program's by a relative error of at most 0.0058.
Values may be sent and summed in bfloat16 or wider, within the bound.
A program may use at most 128 MiB of HBM per device.

```python
import math
import jax
import jax.numpy as jnp
from jax import lax

W = 256
ENC = 128
APP = 48
CODES = 2048
SAMPLES = 96
RAY_DEV = 64
CELLS = 32
ROWS_DEV = 6144
RAYS = 1024
ROWS = 98304
CAP = 192
N_CELL = 16


def draw_dispatch(key, part):
    key = jax.random.fold_in(key, 7)
    device_keys = jax.random.split(key, N_CELL)
    orders = jax.vmap(lambda single: jax.random.permutation(single, ROWS_DEV))(device_keys)
    return orders.reshape(N_CELL * CELLS, CAP).astype(jnp.int32)


def draw_counts(key, part):
    key = jax.random.fold_in(key, 11)
    first_key, second_key, third_key = jax.random.split(key, 3)
    first_draw = jax.random.randint(first_key, (N_CELL, CELLS), 0, CAP + 1)
    second_draw = jax.random.randint(second_key, (N_CELL, CELLS), 0, CAP + 1)
    loads = jnp.maximum(first_draw, second_draw)
    hottest = jax.random.randint(third_key, (), 0, CELLS)
    loads = jnp.where(jnp.arange(CELLS)[None, :] == hottest, CAP, loads)
    return loads.reshape(N_CELL * CELLS).astype(jnp.int32)


def plant(values, key, smallest, top_value):
    longest = values.shape.index(max(values.shape))
    spots = []
    for shift in (0, 1):
        where = [jax.random.randint(jax.random.fold_in(key, axis), (), 0, length) for axis, length in enumerate(values.shape)]
        where[longest] = (where[longest] + shift) % values.shape[longest]
        spots.append(tuple(where))
    return values.at[spots[0]].set(smallest).at[spots[1]].set(top_value)


def levels(own_key, shape, pieces, least, largest):
    gain, own = 1.0, jax.random.fold_in(own_key, 6)
    for axis_at, blocks in pieces:
        steps = jnp.exp(jax.random.uniform(jax.random.fold_in(own, axis_at), (blocks,), jnp.float32, least / len(pieces), largest / len(pieces)))
        gain = gain * jnp.repeat(steps, shape[axis_at] // blocks).reshape([-1 if axis == axis_at else 1 for axis in range(len(shape))])
    return gain


def bell_draw(key, shape, width, limit, pieces=(), held_as=jnp.bfloat16):
    array = width * jax.random.normal(key, shape, jnp.float32)
    if pieces:
        array = array * levels(key, shape, pieces, -0.22, 0.18)
    return jnp.clip(array, -limit, limit).astype(held_as)


def setup_inputs(seed: int = 0, part: int = 0) -> dict:
    streams_of = jax.random.split(jax.random.key(seed), 16)
    own_keys = jax.random.split(jax.random.fold_in(streams_of[15], part), 16)
    positions = jnp.clip(jax.random.uniform(own_keys[0], (3, ROWS), jnp.float32, -1.0, 1.0) * levels(own_keys[0], (3, ROWS), ((1, 16),), -0.4, 0.0), -1.0, 1.0)
    deltas = jnp.clip(jnp.exp(math.log(0.1) - 1.609438 * jax.random.uniform(own_keys[1], (ROWS,), jnp.float32) ** levels(own_keys[1], (ROWS,), ((0, 16),), -0.2, 0.2)), 0.02, 0.1)
    background = jnp.clip(1.0 * jax.random.uniform(own_keys[2], (3, RAYS), jnp.float32) ** levels(own_keys[2], (3, RAYS), ((1, 16),), -0.2, 0.2), 0.0, 1.0)
    target = jnp.clip(1.0 * jax.random.uniform(own_keys[3], (3, RAYS), jnp.float32) ** levels(own_keys[3], (3, RAYS), ((1, 16),), -0.2, 0.2), 0.0, 1.0)
    ray_codes = plant(jax.random.randint(own_keys[4], (RAYS,), 0, CODES), jax.random.fold_in(own_keys[4], 1), 0, CODES - 1).astype(jnp.int32)
    frequencies = bell_draw(streams_of[5], (3, ENC // 2), 4.0, 16.0, (), jnp.float32)
    w_first = bell_draw(streams_of[6], (CELLS, ENC, W), ENC ** -0.5, 0.5, ((0, 16),))
    b_first = bell_draw(streams_of[7], (CELLS, W), 0.5, 3.0, ((0, 16),), jnp.float32)
    w_second = bell_draw(streams_of[8], (CELLS, W, W), W ** -0.5, 0.375, ((0, 16),))
    b_second = bell_draw(streams_of[9], (CELLS, W), 0.5, 3.0, ((0, 16),), jnp.float32)
    head_out = bell_draw(streams_of[10], (CELLS, 4, W), W ** -0.5, 0.375, ((0, 16),))
    head_app = bell_draw(streams_of[11], (CELLS, 3, APP), APP ** -0.5, 0.875, ((0, 16),))
    app_table = bell_draw(streams_of[12], (APP, CODES), 1.0, 5.0, (), jnp.float32)
    dispatch = draw_dispatch(jax.random.fold_in(jax.random.fold_in(streams_of[15], part), 71), part)
    counts = draw_counts(jax.random.fold_in(jax.random.fold_in(streams_of[15], part), 71), part)
    return {"positions": positions, "deltas": deltas, "background": background, "target": target, "ray_codes": ray_codes, "frequencies": frequencies, "w_first": w_first, "b_first": b_first, "w_second": w_second, "b_second": b_second, "head_out": head_out, "head_app": head_app, "app_table": app_table, "dispatch": dispatch, "counts": counts}


loss_scale = 256.0

def encode(coord_x, coord_y, coord_z, frequencies):
    angle_arg = coord_x[..., None] * frequencies[0] + coord_y[..., None] * frequencies[1]
    angle_arg = angle_arg + coord_z[..., None] * frequencies[2]
    return jnp.concatenate([jnp.sin(angle_arg), jnp.cos(angle_arg)], axis=-1).astype(jnp.bfloat16)

def silu_slope(pre_value):
    sigmoid_value = jax.nn.sigmoid(pre_value)
    return sigmoid_value * (1.0 + pre_value * (1.0 - sigmoid_value))

def composite_loss(raw_values, routed, deltas, background, target):
    density = routed * jax.nn.softplus(raw_values[..., 0])
    optical = density * deltas
    running = jnp.cumsum(optical, axis=1)
    before = jnp.concatenate([jnp.zeros_like(optical[:, :1]), running[:, :-1]], axis=1)
    weight = jnp.exp(-before) * (1.0 - jnp.exp(-optical))
    colors = jax.nn.sigmoid(raw_values[..., 1:4])
    pixels = jnp.einsum('rs,rsk->kr', weight, colors) + jnp.exp(-running[:, -1])[None, :] * background
    return loss_scale * 0.5 * jnp.sum((pixels - target) ** 2)

def cell_forward(encoded, code_ids, w_one, b_one, w_two, b_two, head_one, app_one, app_table):
    pre_first = jnp.dot(encoded, w_one, preferred_element_type=jnp.float32) + b_one
    act_first = jax.nn.silu(pre_first).astype(jnp.bfloat16)
    pre_second = jnp.dot(act_first, w_two, preferred_element_type=jnp.float32) + b_two
    act_second = jax.nn.silu(pre_second).astype(jnp.bfloat16)
    outputs = jnp.dot(act_second, head_one.T, preferred_element_type=jnp.float32)
    projected = jnp.dot(app_one.astype(jnp.float32), app_table, precision=lax.Precision.HIGHEST)
    appear = projected[:, code_ids].T
    color_shift = jnp.concatenate([jnp.zeros((outputs.shape[0], 1), jnp.float32), appear], axis=1)
    raw_values = (outputs + color_shift).astype(jnp.bfloat16)
    return (raw_values, pre_first, act_first, pre_second, act_second)

def reference(positions, deltas, background, target, ray_codes, frequencies, w_first, b_first, w_second, b_second, head_out, head_app, app_table, dispatch, counts):
    listed = dispatch.reshape(N_CELL, CELLS, CAP).astype(jnp.int32)
    row_all = (jnp.arange(N_CELL, dtype=jnp.int32) * ROWS_DEV)[:, None, None] + listed
    live_mask = jnp.arange(CAP, dtype=jnp.int32)[None, None, :] < counts.reshape(N_CELL, CELLS)[:, :, None]
    routed = jnp.zeros((N_CELL * ROWS_DEV,), jnp.float32).at[row_all.reshape(-1)].set(live_mask.reshape(-1).astype(jnp.float32))

    def gather_cell(cell_index):
        row_ids = row_all[:, cell_index, :].reshape(-1)
        encoded = encode(positions[0][row_ids], positions[1][row_ids], positions[2][row_ids], frequencies)
        code_ids = ray_codes[row_ids // SAMPLES]
        return (row_ids, encoded, code_ids)

    def forward_cell(cell_index):
        row_ids, encoded, code_ids = gather_cell(cell_index)
        return cell_forward(encoded, code_ids, w_first[cell_index], b_first[cell_index], w_second[cell_index], b_second[cell_index], head_out[cell_index], head_app[cell_index], app_table)[0]
    cell_list = jnp.arange(CELLS, dtype=jnp.int32)
    raw_cells = lax.map(forward_cell, cell_list)
    row_order = jnp.transpose(row_all, (1, 0, 2)).reshape(-1)
    raw_rows = jnp.zeros((N_CELL * ROWS_DEV, 4), jnp.bfloat16).at[row_order].set(raw_cells.reshape(-1, 4))
    ray_total = N_CELL * RAY_DEV
    slope_rows = jax.grad(composite_loss)(raw_rows.astype(jnp.float32).reshape(ray_total, SAMPLES, 4), routed.reshape(ray_total, SAMPLES), deltas.reshape(ray_total, SAMPLES), background, target)
    slope_rows = slope_rows.reshape(-1, 4).astype(jnp.bfloat16)

    def backward_cell(table_total, cell_index):
        row_ids, encoded, code_ids = gather_cell(cell_index)
        w_two = w_second[cell_index]
        head_one = head_out[cell_index]
        app_one = head_app[cell_index]
        produced = cell_forward(encoded, code_ids, w_first[cell_index], b_first[cell_index], w_two, b_second[cell_index], head_one, app_one, app_table)
        pre_first, act_first, pre_second, act_second = (produced[1], produced[2], produced[3], produced[4])
        slopes = slope_rows[row_ids]
        grad_head = jnp.dot(slopes.T, act_second, preferred_element_type=jnp.float32)
        back_second = jnp.dot(slopes, head_one, preferred_element_type=jnp.float32)
        delta_second = (back_second * silu_slope(pre_second)).astype(jnp.bfloat16)
        grad_two = jnp.dot(act_first.T, delta_second, preferred_element_type=jnp.float32)
        grad_bias_two = lax.optimization_barrier(jnp.sum(delta_second.astype(jnp.float32), axis=0))
        back_first = jnp.dot(delta_second, w_two.T, preferred_element_type=jnp.float32)
        delta_first = (back_first * silu_slope(pre_first)).astype(jnp.bfloat16)
        grad_one = jnp.dot(encoded.T, delta_first, preferred_element_type=jnp.float32)
        grad_bias_one = lax.optimization_barrier(jnp.sum(delta_first.astype(jnp.float32), axis=0))
        per_code = jax.ops.segment_sum(slopes[:, 1:4].astype(jnp.float32), code_ids, num_segments=CODES)
        grad_app = jnp.dot(per_code.T, app_table.T, precision=lax.Precision.HIGHEST)
        table_part = jnp.dot(app_one.astype(jnp.float32).T, per_code.T, precision=lax.Precision.HIGHEST)
        return (table_total + table_part, (grad_one, grad_bias_one, grad_two, grad_bias_two, grad_head, grad_app))
    grad_table, grads = lax.scan(backward_cell, jnp.zeros((APP, CODES), jnp.float32), cell_list)
    return (grads[0], grads[1], grads[2], grads[3], grads[4], grads[5], grad_table)
```

```python
import jax
import jax.numpy as jnp
from jax import lax
from jax.experimental import pallas as pl
from jax.experimental.pallas import tpu as pltpu
from jax.sharding import PartitionSpec as P

loss_scale = 256.0
F32 = jnp.float32
BF16 = jnp.bfloat16
HIGH = lax.Precision.HIGHEST
PARAMS = pltpu.CompilerParams(vmem_limit_bytes=48 * 1024 * 1024)


def nn(a, b, precision=None):
    return lax.dot_general(
        a, b, (((1,), (0,)), ((), ())), precision=precision, preferred_element_type=F32
    )


def nt(a, b, precision=None):
    return lax.dot_general(
        a, b, (((1,), (1,)), ((), ())), precision=precision, preferred_element_type=F32
    )


def tn(a, b, precision=None):
    return lax.dot_general(
        a, b, (((0,), (0,)), ((), ())), precision=precision, preferred_element_type=F32
    )


def chunk_of(total, most):
    best = total
    for size in range(128, most + 1, 128):
        if total % size == 0:
            best = size
    return best


def split3(value):
    high = value.astype(BF16)
    rest = value - high.astype(F32)
    mid = rest.astype(BF16)
    low = (rest - mid.astype(F32)).astype(BF16)
    return high, mid, low


def one_hot(index_row, depth):
    rows = lax.broadcasted_iota(jnp.int32, (depth, index_row.shape[1]), 0)
    return rows == index_row


def hot_bf16(mask):
    return jnp.where(mask, 1.0, 0.0).astype(BF16)


def sigmoid(value):
    return 0.5 * jnp.tanh(0.5 * value) + 0.5


PI_A = 3.140625
PI_B = 9.676535897932e-4


def sine(angle, shift):
    turns = jnp.round(angle * 0.3183098861837907 + shift)
    whole = turns - shift
    rest = (angle - whole * PI_A) - whole * PI_B
    odd = turns - 2.0 * jnp.floor(turns * 0.5)
    rest = rest * (1.0 - 2.0 * odd)
    square = rest * rest
    poly = -2.5052108e-8
    poly = poly * square + 2.7557319e-6
    poly = poly * square - 1.9841270e-4
    poly = poly * square + 8.3333333e-3
    poly = poly * square - 1.6666667e-1
    return rest + rest * square * poly


def pick_kernel(ray_ref, sam_ref, pos_ref, codes_ref, table_ref, slot_ref, app_ref):
    samples = pos_ref.shape[1]
    rays = pos_ref.shape[2]
    slots = ray_ref.shape[1]
    chunk = chunk_of(slots, 1024)
    codes_total = table_ref.shape[1]
    stacked = pos_ref[...].reshape(3 * samples, rays)
    parts = split3(stacked)
    code_hot = jnp.where(one_hot(codes_ref[...], codes_total), 1.0, 0.0).astype(BF16)
    table_parts = split3(table_ref[...])
    app_ref[...] = (nn(table_parts[2], code_hot) + nn(table_parts[1], code_hot)) + nn(
        table_parts[0], code_hot
    )

    def body(step, carry):
        here = pl.ds(pl.multiple_of(step * chunk, 128), chunk)
        ray_hot = hot_bf16(one_hot(ray_ref[:, here], rays))
        sam_hot = one_hot(sam_ref[:, here], samples)
        picked = (nn(parts[2], ray_hot) + nn(parts[1], ray_hot)) + nn(parts[0], ray_hot)
        for axis in range(3):
            part = picked[axis * samples : (axis + 1) * samples]
            slot_ref[axis : axis + 1, here] = jnp.sum(
                jnp.where(sam_hot, part, 0.0), axis=0, keepdims=True
            )
        return carry

    lax.fori_loop(0, slots // chunk, body, 0)


def encode_block(pos, freq):
    angle = pos[0:1] * freq[:, 0:1] + pos[1:2] * freq[:, 1:2]
    angle = angle + pos[2:3] * freq[:, 2:3]
    return jnp.concatenate([sine(angle, 0.0), sine(angle, 0.5)], axis=0).astype(BF16)


def network(pos_ref, freq_ref, w1_ref, b1_ref, w2_ref, b2_ref):
    encoded = encode_block(pos_ref[0], freq_ref[...])
    pre_first = tn(w1_ref[0], encoded) + b1_ref[0]
    sig_first = sigmoid(pre_first)
    act_first = (pre_first * sig_first).astype(BF16)
    pre_second = tn(w2_ref[0], act_first) + b2_ref[0]
    sig_second = sigmoid(pre_second)
    act_second = (pre_second * sig_second).astype(BF16)
    return encoded, pre_first, sig_first, act_first, pre_second, sig_second, act_second


def forward_kernel(pos_ref, freq_ref, w1_ref, b1_ref, w2_ref, b2_ref, head_ref, out_ref):
    act_second = network(pos_ref, freq_ref, w1_ref, b1_ref, w2_ref, b2_ref)[6]
    out_ref[0] = nn(head_ref[0], act_second)


def backward_kernel(
    pos_ref,
    freq_ref,
    w1_ref,
    b1_ref,
    w2_ref,
    b2_ref,
    head_ref,
    slope_ref,
    gw1_ref,
    gb1_ref,
    gw2_ref,
    gb2_ref,
    gh_ref,
):
    encoded, pre_first, sig_first, act_first, pre_second, sig_second, act_second = network(
        pos_ref, freq_ref, w1_ref, b1_ref, w2_ref, b2_ref
    )
    slopes = slope_ref[0].astype(BF16)

    @pl.when(pl.program_id(1) == 0)
    def _():
        for ref in (gw1_ref, gb1_ref, gw2_ref, gb2_ref, gh_ref):
            ref[...] = jnp.zeros_like(ref)

    ones = jnp.ones((8, slopes.shape[1]), BF16)
    gh_ref[0] += nt(slopes, act_second)
    back_second = tn(head_ref[0], slopes)
    delta_second = (
        back_second * (sig_second * (1.0 + pre_second * (1.0 - sig_second)))
    ).astype(BF16)
    gw2_ref[0] += nt(act_first, delta_second)
    gb2_ref[0] += nt(ones, delta_second)[0:1]
    back_first = nn(w2_ref[0], delta_second)
    delta_first = (back_first * (sig_first * (1.0 + pre_first * (1.0 - sig_first)))).astype(BF16)
    gw1_ref[0] += nt(encoded, delta_first)
    gb1_ref[0] += nt(ones, delta_first)[0:1]


def ray_kernel(
    ray_ref,
    sam_ref,
    cell_ref,
    live_ref,
    outs_ref,
    heads_ref,
    app_ref,
    deltas_ref,
    back_ref,
    target_ref,
    slope_ref,
    partial_ref,
    code_ref,
    shift_ref,
    rows_ref,
    sums_ref,
):
    samples, rays = deltas_ref.shape
    slots = ray_ref.shape[1]
    cells = heads_ref.shape[0] // 3
    chunk = chunk_of(slots, 512)
    steps = slots // chunk
    shift_ref[...] = nn(heads_ref[...], app_ref[...], HIGH)
    rows_ref[...] = jnp.zeros_like(rows_ref)
    shift_parts = split3(shift_ref[...])

    def gather_rows(step, carry):
        here = pl.ds(pl.multiple_of(step * chunk, 128), chunk)
        ray_hot = hot_bf16(one_hot(ray_ref[:, here], rays))
        sam_hot = one_hot(sam_ref[:, here], samples)
        cell_hot = one_hot(cell_ref[:, here], cells)
        shifts = (nn(shift_parts[2], ray_hot) + nn(shift_parts[1], ray_hot)) + nn(
            shift_parts[0], ray_hot
        )
        columns = [outs_ref[0:1, here]]
        for k in range(3):
            part = shifts[k * cells : (k + 1) * cells]
            picked = jnp.sum(jnp.where(cell_hot, part, 0.0), axis=0, keepdims=True)
            columns.append(outs_ref[k + 1 : k + 2, here] + picked)
        columns.append(live_ref[:, here])
        spread = [jnp.where(sam_hot, column, 0.0).astype(BF16) for column in columns]
        rows_ref[...] += nt(jnp.concatenate(spread, axis=0), ray_hot)
        return carry

    lax.fori_loop(0, steps, gather_rows, 0)
    raw = [rows_ref[k * samples : (k + 1) * samples] for k in range(4)]
    routed = rows_ref[4 * samples : 5 * samples]
    deltas = deltas_ref[...]
    first = lax.broadcasted_iota(jnp.int32, (samples, samples), 0)
    second = lax.broadcasted_iota(jnp.int32, (samples, samples), 1)
    earlier = jnp.where(second < first, 1.0, 0.0)
    later = jnp.where(second > first, 1.0, 0.0)
    tail = jnp.exp(-jnp.abs(raw[0]))
    softplus = jnp.maximum(raw[0], 0.0) + jnp.log1p(tail)
    optical = routed * softplus * deltas
    before = nn(earlier, optical, HIGH)
    total = jnp.sum(optical, axis=0, keepdims=True)
    through = jnp.exp(-before)
    kept = jnp.exp(-optical)
    weight = through * (1.0 - kept)
    leaving = jnp.exp(-total)
    back_slope = jnp.zeros_like(total)
    weight_slope = jnp.zeros_like(weight)
    slope_parts = []
    for k in range(3):
        color = jax.nn.sigmoid(raw[k + 1])
        pixel = jnp.sum(weight * color, axis=0, keepdims=True) + leaving * back_ref[k : k + 1]
        pixel_slope = loss_scale * (pixel - target_ref[k : k + 1])
        back_slope = back_slope + pixel_slope * back_ref[k : k + 1]
        weight_slope = weight_slope + pixel_slope * color
        slope_parts.append((weight * pixel_slope * (color * (1.0 - color))).astype(BF16))
    after = nn(later, weight_slope * weight, HIGH)
    optical_slope = weight_slope * through * kept - after - leaving * back_slope
    density_slope = optical_slope * deltas * routed * jax.nn.sigmoid(raw[0])
    stacked = jnp.concatenate([density_slope.astype(BF16)] + slope_parts, axis=0)
    sums_ref[...] = jnp.zeros_like(sums_ref)

    def spread_slopes(step, carry):
        here = pl.ds(pl.multiple_of(step * chunk, 128), chunk)
        ray_hot = hot_bf16(one_hot(ray_ref[:, here], rays))
        sam_hot = one_hot(sam_ref[:, here], samples)
        cell_hot = one_hot(cell_ref[:, here], cells)
        picked = nn(stacked, ray_hot)
        spread = []
        for k in range(4):
            part = picked[k * samples : (k + 1) * samples]
            column = jnp.sum(jnp.where(sam_hot, part, 0.0), axis=0, keepdims=True)
            slope_ref[k : k + 1, here] = column
            if k:
                spread.append(jnp.where(cell_hot, column, 0.0).astype(BF16))
        sums_ref[...] += nt(jnp.concatenate(spread, axis=0), ray_hot)
        return carry

    lax.fori_loop(0, steps, spread_slopes, 0)
    sums = sums_ref[...]
    partial_ref[...] = nt(sums, app_ref[...], HIGH)
    code_ref[...] = tn(heads_ref[...], sums, HIGH)


def table_kernel(codes_ref, terms_ref, out_ref):
    codes_block = out_ref.shape[1]
    base = pl.program_id(0) * codes_block
    rows = lax.broadcasted_iota(jnp.int32, (codes_block, codes_ref.shape[1]), 0) + base
    hot = hot_bf16(rows == codes_ref[...])
    parts = split3(terms_ref[...])
    out_ref[...] = (nt(parts[2], hot) + nt(parts[1], hot)) + nt(parts[0], hot)


def local(
    positions,
    deltas,
    background,
    target,
    ray_codes,
    frequencies,
    w_first,
    b_first,
    w_second,
    b_second,
    head_out,
    head_app,
    app_table,
    dispatch,
    counts,
):
    owners = lax.axis_size("cell")
    lists, capacity = dispatch.shape
    cell_dev, encoding, width = w_first.shape
    rows_local = positions.shape[1]
    rays = ray_codes.shape[0]
    samples = rows_local // rays
    app_width, codes_total = app_table.shape
    slots_cell = owners * capacity

    listed = dispatch.reshape(1, rows_local)
    slot_ray = listed // samples
    slot_sam = listed - slot_ray * samples
    slot_cell = lax.broadcasted_iota(jnp.int32, (lists, capacity), 0).reshape(1, rows_local)
    live = (jnp.arange(capacity, dtype=jnp.int32)[None, :] < counts[:, None]).astype(F32)
    live = live.reshape(1, rows_local)
    pos_grid = jnp.transpose(positions.reshape(3, rays, samples), (0, 2, 1))
    delta_grid = deltas.reshape(rays, samples).T

    slot_pos, app_rows = pl.pallas_call(
        pick_kernel,
        out_shape=(
            jax.ShapeDtypeStruct((3, rows_local), F32),
            jax.ShapeDtypeStruct((app_width, rays), F32),
        ),
        compiler_params=PARAMS,
        name="pick",
    )(slot_ray, slot_sam, pos_grid, ray_codes.reshape(1, rays), app_table)

    per_owner = cell_dev * capacity
    send = jnp.transpose(slot_pos.reshape(3, owners, per_owner), (1, 0, 2))
    extra = jnp.concatenate([head_app.astype(F32).reshape(-1), ray_codes.astype(F32)])
    extra = jnp.broadcast_to(extra[None, :], (owners, extra.shape[0]))
    message = jnp.concatenate([send.reshape(owners, 3 * per_owner), extra], axis=1)
    message = lax.all_to_all(message, "cell", split_axis=0, concat_axis=0, tiled=True)
    cell_pos = message[:, : 3 * per_owner].reshape(owners, 3, cell_dev, capacity)
    cell_pos = jnp.transpose(cell_pos, (2, 1, 0, 3)).reshape(cell_dev, 3, slots_cell)
    head_size = cell_dev * 3 * app_width
    heads = message[:, 3 * per_owner : 3 * per_owner + head_size]
    heads = jnp.transpose(heads.reshape(lists, 3, app_width), (1, 0, 2)).reshape(-1, app_width)
    all_codes = message[:, 3 * per_owner + head_size :].astype(jnp.int32).reshape(1, owners * rays)

    chunk = chunk_of(slots_cell, 1024)
    grid = (cell_dev, slots_cell // chunk)
    half = frequencies.shape[1]
    freq_columns = frequencies.T
    net_specs = [
        pl.BlockSpec((1, 3, chunk), lambda j, i: (j, 0, i)),
        pl.BlockSpec((half, 3), lambda j, i: (0, 0)),
        pl.BlockSpec((1, encoding, width), lambda j, i: (j, 0, 0)),
        pl.BlockSpec((1, width, 1), lambda j, i: (j, 0, 0)),
        pl.BlockSpec((1, width, width), lambda j, i: (j, 0, 0)),
        pl.BlockSpec((1, width, 1), lambda j, i: (j, 0, 0)),
        pl.BlockSpec((1, 4, width), lambda j, i: (j, 0, 0)),
    ]
    net_args = (
        cell_pos,
        freq_columns,
        w_first,
        b_first[:, :, None],
        w_second,
        b_second[:, :, None],
        head_out,
    )
    outputs = pl.pallas_call(
        forward_kernel,
        grid=grid,
        in_specs=net_specs,
        out_specs=pl.BlockSpec((1, 4, chunk), lambda j, i: (j, 0, i)),
        out_shape=jax.ShapeDtypeStruct((cell_dev, 4, slots_cell), F32),
        compiler_params=PARAMS,
        name="forward",
    )(*net_args)
    outputs = jnp.transpose(outputs.reshape(cell_dev, 4, owners, capacity), (2, 1, 0, 3))
    outputs = outputs.reshape(owners, 4 * per_owner)
    outputs = lax.all_to_all(outputs, "cell", split_axis=0, concat_axis=0, tiled=True)
    slot_outs = jnp.transpose(outputs.reshape(owners, 4, per_owner), (1, 0, 2))
    slot_outs = slot_outs.reshape(4, rows_local)

    slopes, partial, code_terms = pl.pallas_call(
        ray_kernel,
        out_shape=(
            jax.ShapeDtypeStruct((4, rows_local), F32),
            jax.ShapeDtypeStruct((3 * lists, app_width), F32),
            jax.ShapeDtypeStruct((app_width, rays), F32),
        ),
        scratch_shapes=[
            pltpu.VMEM((3 * lists, rays), F32),
            pltpu.VMEM((5 * samples, rays), F32),
            pltpu.VMEM((3 * lists, rays), F32),
        ],
        compiler_params=PARAMS,
        name="rays",
    )(
        slot_ray,
        slot_sam,
        slot_cell,
        live,
        slot_outs,
        heads,
        app_rows,
        delta_grid,
        background,
        target,
    )

    send = jnp.transpose(slopes.reshape(4, owners, per_owner), (1, 0, 2))
    partial = jnp.transpose(partial.reshape(3, lists, app_width), (1, 0, 2))
    message = jnp.concatenate(
        [
            send.reshape(owners, 4 * per_owner),
            partial.reshape(owners, head_size),
            jnp.broadcast_to(code_terms.reshape(1, -1), (owners, app_width * rays)),
        ],
        axis=1,
    )
    message = lax.all_to_all(message, "cell", split_axis=0, concat_axis=0, tiled=True)
    cell_slopes = message[:, : 4 * per_owner].reshape(owners, 4, cell_dev, capacity)
    cell_slopes = jnp.transpose(cell_slopes, (2, 1, 0, 3)).reshape(cell_dev, 4, slots_cell)
    grad_head_app = jnp.sum(message[:, 4 * per_owner : 4 * per_owner + head_size], axis=0)
    grad_head_app = grad_head_app.reshape(cell_dev, 3, app_width)
    terms = message[:, 4 * per_owner + head_size :].reshape(owners, app_width, rays)
    terms = jnp.transpose(terms, (1, 0, 2)).reshape(app_width, owners * rays)

    whole = lambda *dims: pl.BlockSpec((1,) + dims, lambda j, i: (j, 0, 0))
    grad_w_first, grad_b_first, grad_w_second, grad_b_second, grad_head_out = pl.pallas_call(
        backward_kernel,
        grid=grid,
        in_specs=net_specs + [pl.BlockSpec((1, 4, chunk), lambda j, i: (j, 0, i))],
        out_specs=(
            whole(encoding, width),
            whole(1, width),
            whole(width, width),
            whole(1, width),
            whole(4, width),
        ),
        out_shape=(
            jax.ShapeDtypeStruct((cell_dev, encoding, width), F32),
            jax.ShapeDtypeStruct((cell_dev, 1, width), F32),
            jax.ShapeDtypeStruct((cell_dev, width, width), F32),
            jax.ShapeDtypeStruct((cell_dev, 1, width), F32),
            jax.ShapeDtypeStruct((cell_dev, 4, width), F32),
        ),
        compiler_params=PARAMS,
        name="backward",
    )(*net_args, cell_slopes)

    block = chunk_of(codes_total, 512)
    grad_table = pl.pallas_call(
        table_kernel,
        grid=(codes_total // block,),
        in_specs=[
            pl.BlockSpec((1, owners * rays), lambda i: (0, 0)),
            pl.BlockSpec((app_width, owners * rays), lambda i: (0, 0)),
        ],
        out_specs=pl.BlockSpec((app_width, block), lambda i: (0, i)),
        out_shape=jax.ShapeDtypeStruct((app_width, codes_total), F32),
        compiler_params=PARAMS,
        name="table",
    )(all_codes, terms)
    return (
        grad_w_first,
        grad_b_first.reshape(cell_dev, width),
        grad_w_second,
        grad_b_second.reshape(cell_dev, width),
        grad_head_out,
        grad_head_app,
        grad_table,
    )


def solution(mesh):
    placed = (
        P(None, ("groups", "cell")),
        P(("groups", "cell")),
        P(None, ("groups", "cell")),
        P(None, ("groups", "cell")),
        P(("groups", "cell")),
        P(),
        P("cell", None, None),
        P("cell", None),
        P("cell", None, None),
        P("cell", None),
        P("cell", None, None),
        P("cell", None, None),
        P(),
        P(("groups", "cell"), None),
        P(("groups", "cell")),
    )
    return jax.shard_map(
        local,
        mesh=mesh,
        in_specs=placed,
        out_specs=(
            P(("groups", "cell"), None, None),
            P(("groups", "cell"), None),
            P(("groups", "cell"), None, None),
            P(("groups", "cell"), None),
            P(("groups", "cell"), None, None),
            P(("groups", "cell"), None, None),
            P("groups", None),
        ),
        check_vma=False,
    )
```

```python
import functools

import jax
import jax.numpy as jnp
from jax import lax
from jax.experimental import pallas as pl
from jax.experimental.pallas import tpu as pltpu
from jax.sharding import PartitionSpec as P

loss_scale = 256.0
F32 = jnp.float32
BF16 = jnp.bfloat16
HIGH = lax.Precision.HIGHEST
MESH = pl.DeviceIdType.MESH


def nn(a, b, precision=None):
    return lax.dot_general(
        a, b, (((1,), (0,)), ((), ())), precision=precision, preferred_element_type=F32
    )


def nt(a, b, precision=None):
    return lax.dot_general(
        a, b, (((1,), (1,)), ((), ())), precision=precision, preferred_element_type=F32
    )


def tn(a, b, precision=None):
    return lax.dot_general(
        a, b, (((0,), (0,)), ((), ())), precision=precision, preferred_element_type=F32
    )


def chunk_of(total, most):
    best = total
    for size in range(128, most + 1, 128):
        if total % size == 0:
            best = size
    return best


def split3(value):
    high = value.astype(BF16)
    rest = value - high.astype(F32)
    mid = rest.astype(BF16)
    low = (rest - mid.astype(F32)).astype(BF16)
    return high, mid, low


def one_hot(index_row, depth):
    rows = lax.broadcasted_iota(jnp.int32, (depth, index_row.shape[1]), 0)
    return rows == index_row


def hot_bf16(mask):
    return jnp.where(mask, 1.0, 0.0).astype(BF16)


def sigmoid(value):
    return 0.5 * jnp.tanh(0.5 * value) + 0.5


PI_A = 3.140625
PI_B = 9.676535897932e-4


def sine(angle, shift):
    turns = jnp.round(angle * 0.3183098861837907 + shift)
    whole = turns - shift
    rest = (angle - whole * PI_A) - whole * PI_B
    odd = turns - 2.0 * jnp.floor(turns * 0.5)
    rest = rest * (1.0 - 2.0 * odd)
    square = rest * rest
    poly = -2.5052108e-8
    poly = poly * square + 2.7557319e-6
    poly = poly * square - 1.9841270e-4
    poly = poly * square + 8.3333333e-3
    poly = poly * square - 1.6666667e-1
    return rest + rest * square * poly


def start_all(me, owners, source, landing, send_sems, recv_sems):
    def start(step, carry):
        there = lax.rem(me + step, owners)
        pltpu.make_async_remote_copy(
            src_ref=source(there),
            dst_ref=landing.at[me],
            send_sem=send_sems.at[step],
            recv_sem=recv_sems.at[me],
            device_id={"cell": there},
            device_id_type=MESH,
        ).start()
        return carry

    lax.fori_loop(1, owners, start, 0)


def wait_all(me, owners, source, landing, send_sems, recv_sems):
    def wait(step, carry):
        there = lax.rem(me + step, owners)
        copy = pltpu.make_async_remote_copy(
            src_ref=source(there),
            dst_ref=landing.at[there],
            send_sem=send_sems.at[step],
            recv_sem=recv_sems.at[there],
            device_id={"cell": there},
            device_id_type=MESH,
        )
        copy.wait_recv()
        copy.wait_send()
        return carry

    lax.fori_loop(1, owners, wait, 0)


def encode_block(pos, freq):
    angle = pos[0:1] * freq[:, 0:1] + pos[1:2] * freq[:, 1:2]
    angle = angle + pos[2:3] * freq[:, 2:3]
    return jnp.concatenate([sine(angle, 0.0), sine(angle, 0.5)], axis=0).astype(BF16)


def whole_kernel(
    owners,
    capacity,
    ray_ref,
    sam_ref,
    cell_ref,
    live_ref,
    pos_ref,
    codes_ref,
    table_ref,
    extra_ref,
    freq_ref,
    w1_ref,
    b1_ref,
    w2_ref,
    b2_ref,
    head_ref,
    deltas_ref,
    back_ref,
    target_ref,
    gw1_ref,
    gb1_ref,
    gw2_ref,
    gb2_ref,
    gh_ref,
    ga_ref,
    gt_ref,
    extra_land,
    pos_send,
    pos_land,
    out_send,
    out_land,
    slope_send,
    slope_land,
    term_send,
    term_land,
    slot_ref,
    cellpos_ref,
    enc_ref,
    act1_ref,
    act2_ref,
    d1_ref,
    d2_ref,
    cellout_ref,
    cellslope_ref,
    outs_ref,
    slope_ref,
    heads_ref,
    app_ref,
    partial_ref,
    shift_ref,
    rows_ref,
    sums_ref,
    send_sems,
    recv_sems,
):
    me = lax.axis_index("cell")
    barrier = pltpu.get_barrier_semaphore()

    def greet(step, carry):
        pl.semaphore_signal(
            barrier,
            inc=1,
            device_id={"cell": lax.rem(me + step, owners)},
            device_id_type=MESH,
        )
        return carry

    lax.fori_loop(1, owners, greet, 0)

    samples, rays = deltas_ref.shape
    slots = ray_ref.shape[1]
    cells = heads_ref.shape[0] // 3
    cell_dev = w1_ref.shape[0]
    app_width = app_ref.shape[0]
    codes_total = table_ref.shape[1]
    per_owner = cell_dev * capacity
    chunk = chunk_of(slots, 1024)
    steps = slots // chunk

    parts = split3(pos_ref[...].reshape(3 * samples, rays))
    code_hot = hot_bf16(one_hot(codes_ref[...], codes_total))
    table_parts = split3(table_ref[...])
    app_ref[...] = (nn(table_parts[2], code_hot) + nn(table_parts[1], code_hot)) + nn(
        table_parts[0], code_hot
    )

    def pick_rows(step, carry):
        here = pl.ds(pl.multiple_of(step * chunk, 128), chunk)
        ray_hot = hot_bf16(one_hot(ray_ref[:, here], rays))
        sam_hot = one_hot(sam_ref[:, here], samples)
        picked = (nn(parts[2], ray_hot) + nn(parts[1], ray_hot)) + nn(parts[0], ray_hot)
        for axis in range(3):
            part = picked[axis * samples : (axis + 1) * samples]
            slot_ref[axis : axis + 1, here] = jnp.sum(
                jnp.where(sam_hot, part, 0.0), axis=0, keepdims=True
            )
        return carry

    lax.fori_loop(0, steps, pick_rows, 0)
    for n in range(owners):
        pos_send[n] = slot_ref[:, n * per_owner : (n + 1) * per_owner]
    pl.semaphore_wait(barrier, owners - 1)
    pos_args = (me, owners, lambda n: pos_send.at[n], pos_land, send_sems.at[0], recv_sems.at[0])
    start_all(*pos_args)
    extra_args = (me, owners, lambda n: extra_ref, extra_land, send_sems.at[1], recv_sems.at[1])
    start_all(*extra_args)
    pos_land[me] = pos_send[me]
    extra_land[me] = extra_ref[...]
    wait_all(*pos_args)
    for j in range(cell_dev):
        cellpos_ref[j] = jnp.concatenate(
            [pos_land[n][:, j * capacity : (j + 1) * capacity] for n in range(owners)], axis=1
        )

    slots_cell = owners * capacity
    lanes = chunk_of(slots_cell, 1024)
    blocks = slots_cell // lanes

    def forward(step, carry):
        j = step // blocks
        here = pl.ds(pl.multiple_of((step % blocks) * lanes, 128), lanes)
        encoded = encode_block(cellpos_ref[j, :, here], freq_ref[...])
        enc_ref[j, :, here] = encoded
        pre = tn(w1_ref[j], encoded) + b1_ref[j]
        sig = sigmoid(pre)
        act = pre * sig
        d1_ref[j, :, here] = sig + act * (1.0 - sig)
        act = act.astype(BF16)
        act1_ref[j, :, here] = act
        pre = tn(w2_ref[j], act) + b2_ref[j]
        sig = sigmoid(pre)
        act = pre * sig
        d2_ref[j, :, here] = sig + act * (1.0 - sig)
        act = act.astype(BF16)
        act2_ref[j, :, here] = act
        cellout_ref[j, :, here] = nn(head_ref[j], act)
        return carry

    lax.fori_loop(0, cell_dev * blocks, forward, 0)
    outs = [cellout_ref[j] for j in range(cell_dev)]
    for n in range(owners):
        out_send[n] = jnp.concatenate(
            [part[:, n * capacity : (n + 1) * capacity] for part in outs], axis=1
        )
    out_args = (me, owners, lambda n: out_send.at[n], out_land, send_sems.at[2], recv_sems.at[2])
    start_all(*out_args)
    out_land[me] = out_send[me]

    wait_all(*extra_args)

    def place_heads(n, carry):
        for k in range(3):
            heads_ref[pl.ds(k * cells + n * cell_dev, cell_dev), :] = extra_land[
                n, k * cell_dev : (k + 1) * cell_dev, :app_width
            ]
        return carry

    lax.fori_loop(0, owners, place_heads, 0)
    shift_ref[...] = nn(heads_ref[...], app_ref[...], HIGH)
    rows_ref[...] = jnp.zeros_like(rows_ref)
    shift_parts = split3(shift_ref[...])
    wait_all(*out_args)
    for n in range(owners):
        outs_ref[:, n * per_owner : (n + 1) * per_owner] = out_land[n]

    def gather_rows(step, carry):
        here = pl.ds(pl.multiple_of(step * chunk, 128), chunk)
        ray_hot = hot_bf16(one_hot(ray_ref[:, here], rays))
        sam_hot = one_hot(sam_ref[:, here], samples)
        cell_hot = one_hot(cell_ref[:, here], cells)
        shifts = (nn(shift_parts[2], ray_hot) + nn(shift_parts[1], ray_hot)) + nn(
            shift_parts[0], ray_hot
        )
        columns = [outs_ref[0:1, here]]
        for k in range(3):
            part = shifts[k * cells : (k + 1) * cells]
            picked = jnp.sum(jnp.where(cell_hot, part, 0.0), axis=0, keepdims=True)
            columns.append(outs_ref[k + 1 : k + 2, here] + picked)
        columns.append(live_ref[:, here])
        spread = [jnp.where(sam_hot, column, 0.0).astype(BF16) for column in columns]
        rows_ref[...] += nt(jnp.concatenate(spread, axis=0), ray_hot)
        return carry

    lax.fori_loop(0, steps, gather_rows, 0)
    raw = [rows_ref[k * samples : (k + 1) * samples] for k in range(4)]
    routed = rows_ref[4 * samples : 5 * samples]
    deltas = deltas_ref[...]
    first = lax.broadcasted_iota(jnp.int32, (samples, samples), 0)
    second = lax.broadcasted_iota(jnp.int32, (samples, samples), 1)
    earlier = jnp.where(second < first, 1.0, 0.0)
    later = jnp.where(second > first, 1.0, 0.0)
    tail = jnp.exp(-jnp.abs(raw[0]))
    softplus = jnp.maximum(raw[0], 0.0) + jnp.log1p(tail)
    optical = routed * softplus * deltas
    before = nn(earlier, optical, HIGH)
    total = jnp.sum(optical, axis=0, keepdims=True)
    through = jnp.exp(-before)
    kept = jnp.exp(-optical)
    weight = through * (1.0 - kept)
    leaving = jnp.exp(-total)
    back_slope = jnp.zeros_like(total)
    weight_slope = jnp.zeros_like(weight)
    slope_parts = []
    for k in range(3):
        color = jax.nn.sigmoid(raw[k + 1])
        pixel = jnp.sum(weight * color, axis=0, keepdims=True) + leaving * back_ref[k : k + 1]
        pixel_slope = loss_scale * (pixel - target_ref[k : k + 1])
        back_slope = back_slope + pixel_slope * back_ref[k : k + 1]
        weight_slope = weight_slope + pixel_slope * color
        slope_parts.append((weight * pixel_slope * (color * (1.0 - color))).astype(BF16))
    after = nn(later, weight_slope * weight, HIGH)
    optical_slope = weight_slope * through * kept - after - leaving * back_slope
    density_slope = optical_slope * deltas * routed * jax.nn.sigmoid(raw[0])
    stacked = jnp.concatenate([density_slope.astype(BF16)] + slope_parts, axis=0)
    sums_ref[...] = jnp.zeros_like(sums_ref)

    def spread_slopes(step, carry):
        here = pl.ds(pl.multiple_of(step * chunk, 128), chunk)
        ray_hot = hot_bf16(one_hot(ray_ref[:, here], rays))
        sam_hot = one_hot(sam_ref[:, here], samples)
        cell_hot = one_hot(cell_ref[:, here], cells)
        picked = nn(stacked, ray_hot)
        spread = []
        for k in range(4):
            part = picked[k * samples : (k + 1) * samples]
            column = jnp.sum(jnp.where(sam_hot, part, 0.0), axis=0, keepdims=True)
            slope_ref[k : k + 1, here] = column
            if k:
                spread.append(jnp.where(cell_hot, column, 0.0).astype(BF16))
        sums_ref[...] += nt(jnp.concatenate(spread, axis=0), ray_hot)
        return carry

    lax.fori_loop(0, steps, spread_slopes, 0)
    for n in range(owners):
        slope_send[n] = slope_ref[:, n * per_owner : (n + 1) * per_owner]
    slope_args = (
        me,
        owners,
        lambda n: slope_send.at[n],
        slope_land,
        send_sems.at[3],
        recv_sems.at[3],
    )
    start_all(*slope_args)
    slope_land[me] = slope_send[me]
    sums = sums_ref[...]
    partial_ref[...] = nt(sums, app_ref[...], HIGH)
    terms = tn(heads_ref[...], sums, HIGH)

    def place_terms(n, carry):
        term_send[n, :app_width, :rays] = terms
        for k in range(3):
            term_send[
                n, app_width + k * cell_dev : app_width + (k + 1) * cell_dev, :app_width
            ] = partial_ref[pl.ds(k * cells + n * cell_dev, cell_dev), :]
        return carry

    term_send[...] = jnp.zeros_like(term_send)
    lax.fori_loop(0, owners, place_terms, 0)
    term_args = (
        me,
        owners,
        lambda n: term_send.at[n],
        term_land,
        send_sems.at[4],
        recv_sems.at[4],
    )
    wait_all(*slope_args)
    start_all(*term_args)
    term_land[me] = term_send[me]
    for j in range(cell_dev):
        cellslope_ref[j] = jnp.concatenate(
            [slope_land[n][:, j * capacity : (j + 1) * capacity] for n in range(owners)], axis=1
        )

    for ref in (gw1_ref, gb1_ref, gw2_ref, gb2_ref, gh_ref):
        ref[...] = jnp.zeros_like(ref)

    def backward(step, carry):
        j = step // blocks
        here = pl.ds(pl.multiple_of((step % blocks) * lanes, 128), lanes)
        slopes = cellslope_ref[j, :, here].astype(BF16)
        ones = jnp.ones((8, lanes), BF16)
        gh_ref[j] += nt(slopes, act2_ref[j, :, here])
        delta = (tn(head_ref[j], slopes) * d2_ref[j, :, here]).astype(BF16)
        gw2_ref[j] += nt(act1_ref[j, :, here], delta)
        gb2_ref[j] += nt(ones, delta)[0:1]
        delta = (nn(w2_ref[j], delta) * d1_ref[j, :, here]).astype(BF16)
        gw1_ref[j] += nt(enc_ref[j, :, here], delta)
        gb1_ref[j] += nt(ones, delta)[0:1]
        return carry

    lax.fori_loop(0, cell_dev * blocks, backward, 0)

    wait_all(*term_args)
    total = term_land[0]
    for n in range(1, owners):
        total = total + term_land[n]
    ga_ref[...] = total[app_width:, :app_width]
    terms = jnp.concatenate([term_land[n][:app_width, :rays] for n in range(owners)], axis=1)
    code_row = 3 * cell_dev
    all_codes = jnp.concatenate(
        [extra_land[n][code_row : code_row + 1, :rays] for n in range(owners)], axis=1
    ).astype(jnp.int32)
    term_parts = split3(terms)
    block = chunk_of(codes_total, 512)
    for first_code in range(0, codes_total, block):
        hot = hot_bf16(one_hot(all_codes - first_code, block))
        gt_ref[:, first_code : first_code + block] = (
            nt(term_parts[2], hot) + nt(term_parts[1], hot)
        ) + nt(term_parts[0], hot)


def local(
    positions,
    deltas,
    background,
    target,
    ray_codes,
    frequencies,
    w_first,
    b_first,
    w_second,
    b_second,
    head_out,
    head_app,
    app_table,
    dispatch,
    counts,
):
    owners = lax.axis_size("cell")
    lists, capacity = dispatch.shape
    cell_dev, encoding, width = w_first.shape
    rows_local = positions.shape[1]
    rays = ray_codes.shape[0]
    samples = rows_local // rays
    app_width, codes_total = app_table.shape
    slots_cell = owners * capacity

    listed = dispatch.reshape(1, rows_local)
    slot_ray = listed // samples
    slot_sam = listed - slot_ray * samples
    slot_cell = lax.broadcasted_iota(jnp.int32, (lists, capacity), 0).reshape(1, rows_local)
    live = (jnp.arange(capacity, dtype=jnp.int32)[None, :] < counts[:, None]).astype(F32)
    live = live.reshape(1, rows_local)
    pos_grid = jnp.transpose(positions.reshape(3, rays, samples), (0, 2, 1))
    delta_grid = deltas.reshape(rays, samples).T

    per_owner = cell_dev * capacity
    side = max(rays, app_width)
    extra = jnp.transpose(head_app.astype(F32), (1, 0, 2)).reshape(3 * cell_dev, app_width)
    extra = jnp.concatenate(
        [
            jnp.pad(extra, ((0, 0), (0, side - app_width))),
            jnp.pad(ray_codes.astype(F32)[None, :], ((0, 0), (0, side - rays))),
        ],
        axis=0,
    )
    term_rows = app_width + 3 * cell_dev
    in_vmem = pl.BlockSpec(memory_space=pltpu.VMEM)
    outs = (
        jax.ShapeDtypeStruct((cell_dev, encoding, width), F32),
        jax.ShapeDtypeStruct((cell_dev, 1, width), F32),
        jax.ShapeDtypeStruct((cell_dev, width, width), F32),
        jax.ShapeDtypeStruct((cell_dev, 1, width), F32),
        jax.ShapeDtypeStruct((cell_dev, 4, width), F32),
        jax.ShapeDtypeStruct((3 * cell_dev, app_width), F32),
        jax.ShapeDtypeStruct((app_width, codes_total), F32),
    )
    (
        grad_w_first,
        grad_b_first,
        grad_w_second,
        grad_b_second,
        grad_head_out,
        grad_head_app,
        grad_table,
    ) = pl.pallas_call(
        functools.partial(whole_kernel, owners, capacity),
        out_shape=outs,
        in_specs=[in_vmem] * 17,
        out_specs=(in_vmem,) * 7,
        scratch_shapes=[
            pltpu.VMEM((owners,) + extra.shape, F32),
            pltpu.VMEM((owners, 3, per_owner), F32),
            pltpu.VMEM((owners, 3, per_owner), F32),
            pltpu.VMEM((owners, 4, per_owner), F32),
            pltpu.VMEM((owners, 4, per_owner), F32),
            pltpu.VMEM((owners, 4, per_owner), F32),
            pltpu.VMEM((owners, 4, per_owner), F32),
            pltpu.VMEM((owners, term_rows, side), F32),
            pltpu.VMEM((owners, term_rows, side), F32),
            pltpu.VMEM((3, rows_local), F32),
            pltpu.VMEM((cell_dev, 3, slots_cell), F32),
            pltpu.VMEM((cell_dev, encoding, slots_cell), BF16),
            pltpu.VMEM((cell_dev, width, slots_cell), BF16),
            pltpu.VMEM((cell_dev, width, slots_cell), BF16),
            pltpu.VMEM((cell_dev, width, slots_cell), F32),
            pltpu.VMEM((cell_dev, width, slots_cell), F32),
            pltpu.VMEM((cell_dev, 4, slots_cell), F32),
            pltpu.VMEM((cell_dev, 4, slots_cell), F32),
            pltpu.VMEM((4, rows_local), F32),
            pltpu.VMEM((4, rows_local), F32),
            pltpu.VMEM((3 * lists, app_width), F32),
            pltpu.VMEM((app_width, rays), F32),
            pltpu.VMEM((3 * lists, app_width), F32),
            pltpu.VMEM((3 * lists, rays), F32),
            pltpu.VMEM((5 * samples, rays), F32),
            pltpu.VMEM((3 * lists, rays), F32),
            pltpu.SemaphoreType.DMA((5, owners)),
            pltpu.SemaphoreType.DMA((5, owners)),
        ],
        compiler_params=pltpu.CompilerParams(
            vmem_limit_bytes=56 * 1024 * 1024, collective_id=0, has_side_effects=True
        ),
        name="whole",
    )(
        slot_ray,
        slot_sam,
        slot_cell,
        live,
        pos_grid,
        ray_codes.reshape(1, rays),
        app_table,
        extra,
        frequencies.T,
        w_first,
        b_first[:, :, None],
        w_second,
        b_second[:, :, None],
        head_out,
        delta_grid,
        background,
        target,
    )
    grad_head_app = jnp.transpose(grad_head_app.reshape(3, cell_dev, app_width), (1, 0, 2))
    return (
        grad_w_first,
        grad_b_first.reshape(cell_dev, width),
        grad_w_second,
        grad_b_second.reshape(cell_dev, width),
        grad_head_out,
        grad_head_app,
        grad_table,
    )


def solution(mesh):
    placed = (
        P(None, ("groups", "cell")),
        P(("groups", "cell")),
        P(None, ("groups", "cell")),
        P(None, ("groups", "cell")),
        P(("groups", "cell")),
        P(),
        P("cell", None, None),
        P("cell", None),
        P("cell", None, None),
        P("cell", None),
        P("cell", None, None),
        P("cell", None, None),
        P(),
        P(("groups", "cell"), None),
        P(("groups", "cell")),
    )
    return jax.shard_map(
        local,
        mesh=mesh,
        in_specs=placed,
        out_specs=(
            P(("groups", "cell"), None, None),
            P(("groups", "cell"), None),
            P(("groups", "cell"), None, None),
            P(("groups", "cell"), None),
            P(("groups", "cell"), None, None),
            P(("groups", "cell"), None, None),
            P("groups", None),
        ),
        check_vma=False,
    )
```

```python
import functools

import jax
import jax.numpy as jnp
from jax import lax
from jax.experimental import pallas as pl
from jax.experimental.pallas import tpu as pltpu
from jax.sharding import PartitionSpec as P

loss_scale = 256.0
F32 = jnp.float32
BF16 = jnp.bfloat16
HIGH = lax.Precision.HIGHEST
MESH = pl.DeviceIdType.MESH


def nn(a, b, precision=None):
    return lax.dot_general(
        a, b, (((1,), (0,)), ((), ())), precision=precision, preferred_element_type=F32
    )


def nt(a, b, precision=None):
    return lax.dot_general(
        a, b, (((1,), (1,)), ((), ())), precision=precision, preferred_element_type=F32
    )


def tn(a, b, precision=None):
    return lax.dot_general(
        a, b, (((0,), (0,)), ((), ())), precision=precision, preferred_element_type=F32
    )


def chunk_of(total, most):
    best = total
    for size in range(128, most + 1, 128):
        if total % size == 0:
            best = size
    return best


def split3(value):
    high = value.astype(BF16)
    rest = value - high.astype(F32)
    mid = rest.astype(BF16)
    low = (rest - mid.astype(F32)).astype(BF16)
    return high, mid, low


def one_hot(index_row, depth):
    rows = lax.broadcasted_iota(jnp.int32, (depth, index_row.shape[1]), 0)
    return rows == index_row


def hot_bf16(mask):
    return jnp.where(mask, 1.0, 0.0).astype(BF16)


def identity(size):
    first = lax.broadcasted_iota(jnp.int32, (size, size), 0)
    second = lax.broadcasted_iota(jnp.int32, (size, size), 1)
    return jnp.where(first == second, 1.0, 0.0)


def sigmoid(value):
    return 0.5 * jnp.tanh(0.5 * value) + 0.5


PI_A = 3.140625
PI_B = 9.676535897932e-4


def sine(angle, shift):
    turns = jnp.round(angle * 0.3183098861837907 + shift)
    whole = turns - shift
    rest = (angle - whole * PI_A) - whole * PI_B
    odd = turns - 2.0 * jnp.floor(turns * 0.5)
    rest = rest * (1.0 - 2.0 * odd)
    square = rest * rest
    poly = -2.5052108e-8
    poly = poly * square + 2.7557319e-6
    poly = poly * square - 1.9841270e-4
    poly = poly * square + 8.3333333e-3
    poly = poly * square - 1.6666667e-1
    return rest + rest * square * poly


def start_all(me, owners, source, landing, send_sems, recv_sems):
    def start(step, carry):
        there = lax.rem(me + step, owners)
        pltpu.make_async_remote_copy(
            src_ref=source(there),
            dst_ref=landing.at[me],
            send_sem=send_sems.at[step],
            recv_sem=recv_sems.at[me],
            device_id={"cell": there},
            device_id_type=MESH,
        ).start()
        return carry

    lax.fori_loop(1, owners, start, 0)


def wait_all(me, owners, source, landing, send_sems, recv_sems):
    def wait(step, carry):
        there = lax.rem(me + step, owners)
        copy = pltpu.make_async_remote_copy(
            src_ref=source(there),
            dst_ref=landing.at[there],
            send_sem=send_sems.at[step],
            recv_sem=recv_sems.at[there],
            device_id={"cell": there},
            device_id_type=MESH,
        )
        copy.wait_recv()
        copy.wait_send()
        return carry

    lax.fori_loop(1, owners, wait, 0)


def encode_block(pos, freq):
    angle = pos[0:1] * freq[:, 0:1] + pos[1:2] * freq[:, 1:2]
    angle = angle + pos[2:3] * freq[:, 2:3]
    return jnp.concatenate([sine(angle, 0.0), sine(angle, 0.5)], axis=0).astype(BF16)


def whole_kernel(
    owners,
    capacity,
    ray_ref,
    sam_ref,
    counts_ref,
    pos_ref,
    codes_ref,
    table_ref,
    extra_ref,
    freq_ref,
    w1_ref,
    b1_ref,
    w2_ref,
    b2_ref,
    head_ref,
    deltas_ref,
    back_ref,
    target_ref,
    gw1_ref,
    gb1_ref,
    gw2_ref,
    gb2_ref,
    gh_ref,
    ga_ref,
    gt_ref,
    extra_land,
    pos_send,
    pos_land,
    out_send,
    out_land,
    slope_send,
    slope_land,
    term_send,
    term_land,
    slot_ref,
    cellpos_ref,
    enc_ref,
    act1_ref,
    act2_ref,
    d1_ref,
    d2_ref,
    cellout_ref,
    cellslope_ref,
    outs_ref,
    slope_ref,
    heads_ref,
    app_ref,
    partial_ref,
    shift_ref,
    rows_ref,
    sums_ref,
    freqcol_ref,
    b1col_ref,
    b2col_ref,
    hot_ref,
    send_sems,
    recv_sems,
):
    me = lax.axis_index("cell")
    barrier = pltpu.get_barrier_semaphore()

    def greet(step, carry):
        pl.semaphore_signal(
            barrier,
            inc=1,
            device_id={"cell": lax.rem(me + step, owners)},
            device_id_type=MESH,
        )
        return carry

    lax.fori_loop(1, owners, greet, 0)

    samples, rays = deltas_ref.shape
    slots = ray_ref.shape[1]
    cells = heads_ref.shape[0] // 3
    cell_dev = w1_ref.shape[0]
    app_width = app_ref.shape[0]
    codes_total = table_ref.shape[1]
    per_owner = cell_dev * capacity
    chunk = chunk_of(slots, 1024)
    steps = slots // chunk

    parts = jnp.concatenate(split3(pos_ref[...].reshape(3 * samples, rays)), axis=1)

    def pick_rows(step, carry):
        here = pl.ds(pl.multiple_of(step * chunk, 128), chunk)
        ray_hot = hot_bf16(one_hot(ray_ref[:, here], rays))
        sam_hot = one_hot(sam_ref[:, here], samples)
        picked = nn(parts, jnp.concatenate([ray_hot] * 3, axis=0))
        for axis in range(3):
            part = picked[axis * samples : (axis + 1) * samples]
            slot_ref[axis : axis + 1, here] = jnp.sum(
                jnp.where(sam_hot, part, 0.0), axis=0, keepdims=True
            )
        return carry

    lax.fori_loop(0, steps, pick_rows, 0)
    for n in range(owners):
        pos_send[n] = slot_ref[:, n * per_owner : (n + 1) * per_owner]
    pl.semaphore_wait(barrier, owners - 1)
    pos_args = (me, owners, lambda n: pos_send.at[n], pos_land, send_sems.at[0], recv_sems.at[0])
    start_all(*pos_args)
    extra_args = (me, owners, lambda n: extra_ref, extra_land, send_sems.at[1], recv_sems.at[1])
    start_all(*extra_args)
    pos_land[me] = pos_send[me]
    extra_land[me] = extra_ref[...]

    freqcol_ref[...] = tn(freq_ref[...], identity(3), HIGH)
    for bias_ref, column_ref in ((b1_ref, b1col_ref), (b2_ref, b2col_ref)):
        columns = tn(bias_ref[...], identity(cell_dev), HIGH)
        for j in range(cell_dev):
            column_ref[j] = columns[:, j : j + 1]
    code_hot = hot_bf16(one_hot(codes_ref[...], codes_total))
    table_parts = split3(table_ref[...])
    app_ref[...] = (nn(table_parts[2], code_hot) + nn(table_parts[1], code_hot)) + nn(
        table_parts[0], code_hot
    )
    for ref in (gw1_ref, gb1_ref, gw2_ref, gb2_ref, gh_ref, term_send):
        ref[...] = jnp.zeros_like(ref)
    code_row = 3 * cell_dev

    def codes_of_all():
        return jnp.concatenate(
            [extra_land[n][code_row : code_row + 1, :rays] for n in range(owners)], axis=1
        ).astype(jnp.int32)

    block = chunk_of(codes_total, 512)
    kept_hot = hot_ref.shape[0] == codes_total
    if kept_hot:
        wait_all(*extra_args)
        all_codes = codes_of_all()
        for first_code in range(0, codes_total, block):
            hot_ref[first_code : first_code + block, :] = hot_bf16(
                one_hot(all_codes - first_code, block)
            )
    wait_all(*pos_args)
    for j in range(cell_dev):
        cellpos_ref[j] = jnp.concatenate(
            [pos_land[n][:, j * capacity : (j + 1) * capacity] for n in range(owners)], axis=1
        )

    slots_cell = owners * capacity
    lanes = chunk_of(slots_cell, 1024)
    blocks = slots_cell // lanes

    def forward(step, carry):
        j = step // blocks
        here = pl.ds(pl.multiple_of((step % blocks) * lanes, 128), lanes)
        encoded = encode_block(cellpos_ref[j, :, here], freqcol_ref[...])
        enc_ref[j, :, here] = encoded
        pre = tn(w1_ref[j], encoded) + b1col_ref[j]
        sig = sigmoid(pre)
        act = pre * sig
        d1_ref[j, :, here] = sig + act * (1.0 - sig)
        act = act.astype(BF16)
        act1_ref[j, :, here] = act
        pre = tn(w2_ref[j], act) + b2col_ref[j]
        sig = sigmoid(pre)
        act = pre * sig
        d2_ref[j, :, here] = sig + act * (1.0 - sig)
        act = act.astype(BF16)
        act2_ref[j, :, here] = act
        cellout_ref[j, :, here] = nn(head_ref[j], act)
        return carry

    lax.fori_loop(0, cell_dev * blocks, forward, 0)
    outs = [cellout_ref[j] for j in range(cell_dev)]
    for n in range(owners):
        out_send[n] = jnp.concatenate(
            [part[:, n * capacity : (n + 1) * capacity] for part in outs], axis=1
        )
    out_args = (me, owners, lambda n: out_send.at[n], out_land, send_sems.at[2], recv_sems.at[2])
    start_all(*out_args)
    out_land[me] = out_send[me]

    if not kept_hot:
        wait_all(*extra_args)

    def place_heads(n, carry):
        for k in range(3):
            heads_ref[pl.ds(k * cells + n * cell_dev, cell_dev), :] = extra_land[
                n, k * cell_dev : (k + 1) * cell_dev, :app_width
            ]
        return carry

    lax.fori_loop(0, owners, place_heads, 0)
    shift_ref[...] = nn(heads_ref[...], app_ref[...], HIGH)
    rows_ref[...] = jnp.zeros_like(rows_ref)
    shift_parts = jnp.concatenate(split3(shift_ref[...]), axis=1)
    wait_all(*out_args)
    for n in range(owners):
        outs_ref[:, n * per_owner : (n + 1) * per_owner] = out_land[n]

    counts_col = tn(counts_ref[...].astype(F32), jnp.ones((1, 1), F32), HIGH)
    counts_col = jnp.round(counts_col).astype(jnp.int32)

    def slot_places(step, size):
        first_slot = lax.broadcasted_iota(jnp.int32, (cells, size), 0) * capacity
        return first_slot, lax.broadcasted_iota(jnp.int32, (cells, size), 1) + step * size

    def gather_rows(step, carry):
        here = pl.ds(pl.multiple_of(step * chunk, 128), chunk)
        ray_hot = hot_bf16(one_hot(ray_ref[:, here], rays))
        sam_hot = one_hot(sam_ref[:, here], samples)
        first_slot, slot_id = slot_places(step, chunk)
        cell_hot = (slot_id >= first_slot) & (slot_id < first_slot + capacity)
        shifts = nn(shift_parts, jnp.concatenate([ray_hot] * 3, axis=0))
        columns = [outs_ref[0:1, here]]
        for k in range(3):
            part = shifts[k * cells : (k + 1) * cells]
            picked = jnp.sum(jnp.where(cell_hot, part, 0.0), axis=0, keepdims=True)
            columns.append(outs_ref[k + 1 : k + 2, here] + picked)
        live = (slot_id >= first_slot) & (slot_id < first_slot + counts_col)
        columns.append(jnp.sum(jnp.where(live, 1.0, 0.0), axis=0, keepdims=True))
        spread = [jnp.where(sam_hot, column, 0.0).astype(BF16) for column in columns]
        rows_ref[...] += nt(jnp.concatenate(spread, axis=0), ray_hot)
        return carry

    lax.fori_loop(0, steps, gather_rows, 0)
    raw = [rows_ref[k * samples : (k + 1) * samples] for k in range(4)]
    routed = rows_ref[4 * samples : 5 * samples]
    deltas = deltas_ref[...]
    first = lax.broadcasted_iota(jnp.int32, (samples, samples), 0)
    second = lax.broadcasted_iota(jnp.int32, (samples, samples), 1)
    earlier = jnp.where(second < first, 1.0, 0.0)
    later = jnp.where(second > first, 1.0, 0.0)
    tail = jnp.exp(-jnp.abs(raw[0]))
    softplus = jnp.maximum(raw[0], 0.0) + jnp.log1p(tail)
    optical = routed * softplus * deltas
    before = nn(earlier, optical, HIGH)
    total = jnp.sum(optical, axis=0, keepdims=True)
    through = jnp.exp(-before)
    kept = jnp.exp(-optical)
    weight = through * (1.0 - kept)
    leaving = jnp.exp(-total)
    back_slope = jnp.zeros_like(total)
    weight_slope = jnp.zeros_like(weight)
    slope_parts = []
    for k in range(3):
        color = jax.nn.sigmoid(raw[k + 1])
        pixel = jnp.sum(weight * color, axis=0, keepdims=True) + leaving * back_ref[k : k + 1]
        pixel_slope = loss_scale * (pixel - target_ref[k : k + 1])
        back_slope = back_slope + pixel_slope * back_ref[k : k + 1]
        weight_slope = weight_slope + pixel_slope * color
        slope_parts.append((weight * pixel_slope * (color * (1.0 - color))).astype(BF16))
    after = nn(later, weight_slope * weight, HIGH)
    optical_slope = weight_slope * through * kept - after - leaving * back_slope
    density_slope = optical_slope * deltas * routed * jax.nn.sigmoid(raw[0])
    stacked = jnp.concatenate([density_slope.astype(BF16)] + slope_parts, axis=0)
    sums_ref[...] = jnp.zeros_like(sums_ref)

    def spread_slopes(step, carry):
        here = pl.ds(pl.multiple_of(step * chunk, 128), chunk)
        ray_hot = hot_bf16(one_hot(ray_ref[:, here], rays))
        sam_hot = one_hot(sam_ref[:, here], samples)
        first_slot, slot_id = slot_places(step, chunk)
        cell_hot = (slot_id >= first_slot) & (slot_id < first_slot + capacity)
        picked = nn(stacked, ray_hot)
        spread = []
        for k in range(4):
            part = picked[k * samples : (k + 1) * samples]
            column = jnp.sum(jnp.where(sam_hot, part, 0.0), axis=0, keepdims=True)
            slope_ref[k : k + 1, here] = column
            if k:
                spread.append(jnp.where(cell_hot, column, 0.0).astype(BF16))
        sums_ref[...] += nt(jnp.concatenate(spread, axis=0), ray_hot)
        return carry

    lax.fori_loop(0, steps, spread_slopes, 0)
    for n in range(owners):
        slope_send[n] = slope_ref[:, n * per_owner : (n + 1) * per_owner]
    slope_args = (
        me,
        owners,
        lambda n: slope_send.at[n],
        slope_land,
        send_sems.at[3],
        recv_sems.at[3],
    )
    start_all(*slope_args)
    slope_land[me] = slope_send[me]
    sums = sums_ref[...]
    partial_ref[...] = nt(sums, app_ref[...], HIGH)
    terms = tn(heads_ref[...], sums, HIGH)

    def place_terms(n, carry):
        term_send[n, :app_width, :rays] = terms
        for k in range(3):
            term_send[
                n, app_width + k * cell_dev : app_width + (k + 1) * cell_dev, :app_width
            ] = partial_ref[pl.ds(k * cells + n * cell_dev, cell_dev), :]
        return carry

    lax.fori_loop(0, owners, place_terms, 0)
    term_args = (
        me,
        owners,
        lambda n: term_send.at[n],
        term_land,
        send_sems.at[4],
        recv_sems.at[4],
    )
    wait_all(*slope_args)
    start_all(*term_args)
    term_land[me] = term_send[me]
    for j in range(cell_dev):
        cellslope_ref[j] = jnp.concatenate(
            [slope_land[n][:, j * capacity : (j + 1) * capacity] for n in range(owners)], axis=1
        )

    def backward(step, carry):
        j = step // blocks
        here = pl.ds(pl.multiple_of((step % blocks) * lanes, 128), lanes)
        slopes = cellslope_ref[j, :, here].astype(BF16)
        ones = jnp.ones((8, lanes), BF16)
        gh_ref[j] += nt(slopes, act2_ref[j, :, here])
        delta = (tn(head_ref[j], slopes) * d2_ref[j, :, here]).astype(BF16)
        gw2_ref[j] += nt(act1_ref[j, :, here], delta)
        gb2_ref[pl.ds(j, 1), :] += nt(ones, delta)[0:1]
        delta = (nn(w2_ref[j], delta) * d1_ref[j, :, here]).astype(BF16)
        gw1_ref[j] += nt(enc_ref[j, :, here], delta)
        gb1_ref[pl.ds(j, 1), :] += nt(ones, delta)[0:1]
        return carry

    lax.fori_loop(0, cell_dev * blocks, backward, 0)

    wait_all(*term_args)
    total = term_land[0]
    for n in range(1, owners):
        total = total + term_land[n]
    for j in range(cell_dev):
        for k in range(3):
            row = app_width + k * cell_dev + j
            ga_ref[j, k : k + 1, :] = total[row : row + 1, :app_width]
    terms = jnp.concatenate([term_land[n][:app_width, :rays] for n in range(owners)], axis=1)
    term_parts = jnp.concatenate(split3(terms), axis=0)
    if not kept_hot:
        all_codes = codes_of_all()
    for first_code in range(0, codes_total, block):
        if kept_hot:
            hot = hot_ref[first_code : first_code + block, :]
        else:
            hot = hot_bf16(one_hot(all_codes - first_code, block))
        sums = nt(term_parts, hot)
        gt_ref[:, first_code : first_code + block] = (
            sums[2 * app_width :] + sums[app_width : 2 * app_width]
        ) + sums[:app_width]


def local(
    positions,
    deltas,
    background,
    target,
    ray_codes,
    frequencies,
    w_first,
    b_first,
    w_second,
    b_second,
    head_out,
    head_app,
    app_table,
    dispatch,
    counts,
):
    owners = lax.axis_size("cell")
    lists, capacity = dispatch.shape
    cell_dev, encoding, width = w_first.shape
    rows_local = positions.shape[1]
    rays = ray_codes.shape[0]
    samples = rows_local // rays
    app_width, codes_total = app_table.shape
    slots_cell = owners * capacity

    listed = dispatch.reshape(1, rows_local)
    slot_ray = listed // samples
    slot_sam = listed - slot_ray * samples
    pos_grid = jnp.transpose(positions.reshape(3, rays, samples), (0, 2, 1))
    delta_grid = deltas.reshape(rays, samples).T

    per_owner = cell_dev * capacity
    side = max(rays, app_width)
    extra = jnp.transpose(head_app.astype(F32), (1, 0, 2)).reshape(3 * cell_dev, app_width)
    extra = jnp.concatenate(
        [
            jnp.pad(extra, ((0, 0), (0, side - app_width))),
            jnp.pad(ray_codes.astype(F32)[None, :], ((0, 0), (0, side - rays))),
        ],
        axis=0,
    )
    term_rows = app_width + 3 * cell_dev
    hot_rows = codes_total if owners * rays <= 2048 else 16
    in_vmem = pl.BlockSpec(memory_space=pltpu.VMEM)
    outs = (
        jax.ShapeDtypeStruct((cell_dev, encoding, width), F32),
        jax.ShapeDtypeStruct((cell_dev, width), F32),
        jax.ShapeDtypeStruct((cell_dev, width, width), F32),
        jax.ShapeDtypeStruct((cell_dev, width), F32),
        jax.ShapeDtypeStruct((cell_dev, 4, width), F32),
        jax.ShapeDtypeStruct((cell_dev, 3, app_width), F32),
        jax.ShapeDtypeStruct((app_width, codes_total), F32),
    )
    (
        grad_w_first,
        grad_b_first,
        grad_w_second,
        grad_b_second,
        grad_head_out,
        grad_head_app,
        grad_table,
    ) = pl.pallas_call(
        functools.partial(whole_kernel, owners, capacity),
        out_shape=outs,
        in_specs=[in_vmem] * 16,
        out_specs=(in_vmem,) * 7,
        scratch_shapes=[
            pltpu.VMEM((owners,) + extra.shape, F32),
            pltpu.VMEM((owners, 3, per_owner), F32),
            pltpu.VMEM((owners, 3, per_owner), F32),
            pltpu.VMEM((owners, 4, per_owner), F32),
            pltpu.VMEM((owners, 4, per_owner), F32),
            pltpu.VMEM((owners, 4, per_owner), F32),
            pltpu.VMEM((owners, 4, per_owner), F32),
            pltpu.VMEM((owners, term_rows, side), F32),
            pltpu.VMEM((owners, term_rows, side), F32),
            pltpu.VMEM((3, rows_local), F32),
            pltpu.VMEM((cell_dev, 3, slots_cell), F32),
            pltpu.VMEM((cell_dev, encoding, slots_cell), BF16),
            pltpu.VMEM((cell_dev, width, slots_cell), BF16),
            pltpu.VMEM((cell_dev, width, slots_cell), BF16),
            pltpu.VMEM((cell_dev, width, slots_cell), F32),
            pltpu.VMEM((cell_dev, width, slots_cell), F32),
            pltpu.VMEM((cell_dev, 4, slots_cell), F32),
            pltpu.VMEM((cell_dev, 4, slots_cell), F32),
            pltpu.VMEM((4, rows_local), F32),
            pltpu.VMEM((4, rows_local), F32),
            pltpu.VMEM((3 * lists, app_width), F32),
            pltpu.VMEM((app_width, rays), F32),
            pltpu.VMEM((3 * lists, app_width), F32),
            pltpu.VMEM((3 * lists, rays), F32),
            pltpu.VMEM((5 * samples, rays), F32),
            pltpu.VMEM((3 * lists, rays), F32),
            pltpu.VMEM((frequencies.shape[1], 3), F32),
            pltpu.VMEM((cell_dev, width, 1), F32),
            pltpu.VMEM((cell_dev, width, 1), F32),
            pltpu.VMEM((hot_rows, owners * rays), BF16),
            pltpu.SemaphoreType.DMA((5, owners)),
            pltpu.SemaphoreType.DMA((5, owners)),
        ],
        compiler_params=pltpu.CompilerParams(
            vmem_limit_bytes=56 * 1024 * 1024, collective_id=0, has_side_effects=True
        ),
        name="whole",
    )(
        slot_ray,
        slot_sam,
        counts.reshape(1, lists),
        pos_grid,
        ray_codes.reshape(1, rays),
        app_table,
        extra,
        frequencies,
        w_first,
        b_first,
        w_second,
        b_second,
        head_out,
        delta_grid,
        background,
        target,
    )
    return (
        grad_w_first,
        grad_b_first,
        grad_w_second,
        grad_b_second,
        grad_head_out,
        grad_head_app,
        grad_table,
    )


def solution(mesh):
    placed = (
        P(None, ("groups", "cell")),
        P(("groups", "cell")),
        P(None, ("groups", "cell")),
        P(None, ("groups", "cell")),
        P(("groups", "cell")),
        P(),
        P("cell", None, None),
        P("cell", None),
        P("cell", None, None),
        P("cell", None),
        P("cell", None, None),
        P("cell", None, None),
        P(),
        P(("groups", "cell"), None),
        P(("groups", "cell")),
    )
    return jax.shard_map(
        local,
        mesh=mesh,
        in_specs=placed,
        out_specs=(
            P(("groups", "cell"), None, None),
            P(("groups", "cell"), None),
            P(("groups", "cell"), None, None),
            P(("groups", "cell"), None),
            P(("groups", "cell"), None, None),
            P(("groups", "cell"), None, None),
            P("groups", None),
        ),
        check_vma=False,
    )
```

```python
import functools

import jax
import jax.numpy as jnp
from jax import lax
from jax.experimental import pallas as pl
from jax.experimental.pallas import tpu as pltpu
from jax.sharding import PartitionSpec as P

loss_scale = 256.0
F32 = jnp.float32
BF16 = jnp.bfloat16
HIGH = lax.Precision.HIGHEST
MESH = pl.DeviceIdType.MESH


def nn(a, b, precision=None):
    return lax.dot_general(
        a, b, (((1,), (0,)), ((), ())), precision=precision, preferred_element_type=F32
    )


def nt(a, b, precision=None):
    return lax.dot_general(
        a, b, (((1,), (1,)), ((), ())), precision=precision, preferred_element_type=F32
    )


def tn(a, b, precision=None):
    return lax.dot_general(
        a, b, (((0,), (0,)), ((), ())), precision=precision, preferred_element_type=F32
    )


def chunk_of(total, most):
    best = total
    for size in range(128, most + 1, 128):
        if total % size == 0:
            best = size
    return best


def split3(value):
    high = value.astype(BF16)
    rest = value - high.astype(F32)
    mid = rest.astype(BF16)
    low = (rest - mid.astype(F32)).astype(BF16)
    return high, mid, low


def one_hot(index_row, depth):
    rows = lax.broadcasted_iota(jnp.int32, (depth, index_row.shape[1]), 0)
    return rows == index_row


def hot_bf16(mask):
    return jnp.where(mask, 1.0, 0.0).astype(BF16)


def in_pairs(steps, body):
    width = 2 if steps % 2 == 0 else 1

    def several(step, carry):
        for part in range(width):
            carry = body(step * width + part, carry)
        return carry

    lax.fori_loop(0, steps // width, several, 0)


def identity(size):
    first = lax.broadcasted_iota(jnp.int32, (size, size), 0)
    second = lax.broadcasted_iota(jnp.int32, (size, size), 1)
    return jnp.where(first == second, 1.0, 0.0)


def sigmoid(value):
    return 0.5 * jnp.tanh(0.5 * value) + 0.5


PI_A = 3.140625
PI_B = 9.676535897932e-4


def sine(angle, shift):
    turns = jnp.round(angle * 0.3183098861837907 + shift)
    whole = turns - shift
    rest = (angle - whole * PI_A) - whole * PI_B
    odd = turns - 2.0 * jnp.floor(turns * 0.5)
    rest = rest * (1.0 - 2.0 * odd)
    square = rest * rest
    poly = -2.5052108e-8
    poly = poly * square + 2.7557319e-6
    poly = poly * square - 1.9841270e-4
    poly = poly * square + 8.3333333e-3
    poly = poly * square - 1.6666667e-1
    return rest + rest * square * poly


def start_all(me, owners, source, landing, send_sems, recv_sems):
    def start(step, carry):
        there = lax.rem(me + step, owners)
        pltpu.make_async_remote_copy(
            src_ref=source(there),
            dst_ref=landing.at[me],
            send_sem=send_sems.at[step],
            recv_sem=recv_sems.at[me],
            device_id={"cell": there},
            device_id_type=MESH,
        ).start()
        return carry

    lax.fori_loop(1, owners, start, 0)


def wait_all(me, owners, source, landing, send_sems, recv_sems):
    def wait(step, carry):
        there = lax.rem(me + step, owners)
        copy = pltpu.make_async_remote_copy(
            src_ref=source(there),
            dst_ref=landing.at[there],
            send_sem=send_sems.at[step],
            recv_sem=recv_sems.at[there],
            device_id={"cell": there},
            device_id_type=MESH,
        )
        copy.wait_recv()
        copy.wait_send()
        return carry

    lax.fori_loop(1, owners, wait, 0)


def encode_block(pos, freq):
    angle = pos[0:1] * freq[:, 0:1] + pos[1:2] * freq[:, 1:2]
    angle = angle + pos[2:3] * freq[:, 2:3]
    return jnp.concatenate([sine(angle, 0.0), sine(angle, 0.5)], axis=0).astype(BF16)


def whole_kernel(
    owners,
    capacity,
    ray_ref,
    sam_ref,
    counts_ref,
    pos_ref,
    codes_ref,
    table_ref,
    extra_ref,
    freq_ref,
    w1_ref,
    b1_ref,
    w2_ref,
    b2_ref,
    head_ref,
    deltas_ref,
    back_ref,
    target_ref,
    gw1_ref,
    gb1_ref,
    gw2_ref,
    gb2_ref,
    gh_ref,
    ga_ref,
    gt_ref,
    extra_land,
    pos_send,
    pos_land,
    out_send,
    out_land,
    slope_send,
    slope_land,
    term_send,
    term_land,
    slot_ref,
    cellpos_ref,
    enc_ref,
    act1_ref,
    act2_ref,
    d1_ref,
    d2_ref,
    cellout_ref,
    cellslope_ref,
    outs_ref,
    slope_ref,
    heads_ref,
    app_ref,
    partial_ref,
    shift_ref,
    rows_ref,
    sums_ref,
    freqcol_ref,
    b1col_ref,
    b2col_ref,
    hot_ref,
    send_sems,
    recv_sems,
):
    me = lax.axis_index("cell")
    barrier = pltpu.get_barrier_semaphore()

    def greet(step, carry):
        pl.semaphore_signal(
            barrier,
            inc=1,
            device_id={"cell": lax.rem(me + step, owners)},
            device_id_type=MESH,
        )
        return carry

    lax.fori_loop(1, owners, greet, 0)

    samples, rays = deltas_ref.shape
    slots = ray_ref.shape[1]
    cells = heads_ref.shape[0] // 3
    cell_dev = w1_ref.shape[0]
    app_width = app_ref.shape[0]
    codes_total = table_ref.shape[1]
    per_owner = cell_dev * capacity
    chunk = chunk_of(slots, 1024)
    steps = slots // chunk

    parts = jnp.concatenate(split3(pos_ref[...].reshape(3 * samples, rays)), axis=1)

    def pick_rows(step, carry):
        here = pl.ds(pl.multiple_of(step * chunk, 128), chunk)
        ray_hot = hot_bf16(one_hot(ray_ref[:, here], rays))
        sam_hot = one_hot(sam_ref[:, here], samples)
        picked = nn(parts, jnp.concatenate([ray_hot] * 3, axis=0))
        for axis in range(3):
            part = picked[axis * samples : (axis + 1) * samples]
            slot_ref[axis : axis + 1, here] = jnp.sum(
                jnp.where(sam_hot, part, 0.0), axis=0, keepdims=True
            )
        return carry

    in_pairs(steps, pick_rows)
    for n in range(owners):
        pos_send[n] = slot_ref[:, n * per_owner : (n + 1) * per_owner]
    pl.semaphore_wait(barrier, owners - 1)
    pos_args = (me, owners, lambda n: pos_send.at[n], pos_land, send_sems.at[0], recv_sems.at[0])
    start_all(*pos_args)
    extra_args = (me, owners, lambda n: extra_ref, extra_land, send_sems.at[1], recv_sems.at[1])
    start_all(*extra_args)
    pos_land[me] = pos_send[me]
    extra_land[me] = extra_ref[...]

    freqcol_ref[...] = tn(freq_ref[...], identity(3), HIGH)
    for bias_ref, column_ref in ((b1_ref, b1col_ref), (b2_ref, b2col_ref)):
        columns = tn(bias_ref[...], identity(cell_dev), HIGH)
        for j in range(cell_dev):
            column_ref[j] = columns[:, j : j + 1]
    code_hot = hot_bf16(one_hot(codes_ref[...], codes_total))
    table_parts = split3(table_ref[...])
    app_ref[...] = (nn(table_parts[2], code_hot) + nn(table_parts[1], code_hot)) + nn(
        table_parts[0], code_hot
    )
    for ref in (gw1_ref, gb1_ref, gw2_ref, gb2_ref, gh_ref, term_send):
        ref[...] = jnp.zeros_like(ref)
    code_row = 3 * cell_dev

    def codes_of_all():
        return jnp.concatenate(
            [extra_land[n][code_row : code_row + 1, :rays] for n in range(owners)], axis=1
        ).astype(jnp.int32)

    block = chunk_of(codes_total, 512)
    kept_hot = hot_ref.shape[0] == codes_total
    if kept_hot:
        wait_all(*extra_args)
        all_codes = codes_of_all()
        for first_code in range(0, codes_total, block):
            hot_ref[first_code : first_code + block, :] = hot_bf16(
                one_hot(all_codes - first_code, block)
            )
    wait_all(*pos_args)
    for j in range(cell_dev):
        cellpos_ref[j] = jnp.concatenate(
            [pos_land[n][:, j * capacity : (j + 1) * capacity] for n in range(owners)], axis=1
        )

    slots_cell = owners * capacity
    lanes = chunk_of(slots_cell, 1024)
    blocks = slots_cell // lanes

    def forward(step, carry):
        j = step // blocks
        here = pl.ds(pl.multiple_of((step % blocks) * lanes, 128), lanes)
        encoded = encode_block(cellpos_ref[j, :, here], freqcol_ref[...])
        enc_ref[j, :, here] = encoded
        pre = tn(w1_ref[j], encoded) + b1col_ref[j]
        sig = sigmoid(pre)
        act = pre * sig
        d1_ref[j, :, here] = sig + act * (1.0 - sig)
        act = act.astype(BF16)
        act1_ref[j, :, here] = act
        pre = tn(w2_ref[j], act) + b2col_ref[j]
        sig = sigmoid(pre)
        act = pre * sig
        d2_ref[j, :, here] = sig + act * (1.0 - sig)
        act = act.astype(BF16)
        act2_ref[j, :, here] = act
        cellout_ref[j, :, here] = nn(head_ref[j], act)
        return carry

    in_pairs(cell_dev * blocks, forward)
    outs = [cellout_ref[j] for j in range(cell_dev)]
    for n in range(owners):
        out_send[n] = jnp.concatenate(
            [part[:, n * capacity : (n + 1) * capacity] for part in outs], axis=1
        )
    out_args = (me, owners, lambda n: out_send.at[n], out_land, send_sems.at[2], recv_sems.at[2])
    start_all(*out_args)
    out_land[me] = out_send[me]

    if not kept_hot:
        wait_all(*extra_args)

    def place_heads(n, carry):
        for k in range(3):
            heads_ref[pl.ds(k * cells + n * cell_dev, cell_dev), :] = extra_land[
                n, k * cell_dev : (k + 1) * cell_dev, :app_width
            ]
        return carry

    lax.fori_loop(0, owners, place_heads, 0)
    shift_ref[...] = nn(heads_ref[...], app_ref[...], HIGH)
    rows_ref[...] = jnp.zeros_like(rows_ref)
    shift_parts = jnp.concatenate(split3(shift_ref[...]), axis=1)
    wait_all(*out_args)
    for n in range(owners):
        outs_ref[:, n * per_owner : (n + 1) * per_owner] = out_land[n]

    counts_col = tn(counts_ref[...].astype(F32), jnp.ones((1, 1), F32), HIGH)
    counts_col = jnp.round(counts_col).astype(jnp.int32)

    def slot_places(step, size):
        first_slot = lax.broadcasted_iota(jnp.int32, (cells, size), 0) * capacity
        return first_slot, lax.broadcasted_iota(jnp.int32, (cells, size), 1) + step * size

    def gather_rows(step, carry):
        here = pl.ds(pl.multiple_of(step * chunk, 128), chunk)
        ray_hot = hot_bf16(one_hot(ray_ref[:, here], rays))
        sam_hot = one_hot(sam_ref[:, here], samples)
        first_slot, slot_id = slot_places(step, chunk)
        cell_hot = (slot_id >= first_slot) & (slot_id < first_slot + capacity)
        shifts = nn(shift_parts, jnp.concatenate([ray_hot] * 3, axis=0))
        columns = [outs_ref[0:1, here]]
        for k in range(3):
            part = shifts[k * cells : (k + 1) * cells]
            picked = jnp.sum(jnp.where(cell_hot, part, 0.0), axis=0, keepdims=True)
            columns.append(outs_ref[k + 1 : k + 2, here] + picked)
        live = (slot_id >= first_slot) & (slot_id < first_slot + counts_col)
        columns.append(jnp.sum(jnp.where(live, 1.0, 0.0), axis=0, keepdims=True))
        spread = [jnp.where(sam_hot, column, 0.0).astype(BF16) for column in columns]
        rows_ref[...] += nt(jnp.concatenate(spread, axis=0), ray_hot)
        return carry

    in_pairs(steps, gather_rows)
    raw = [rows_ref[k * samples : (k + 1) * samples] for k in range(4)]
    routed = rows_ref[4 * samples : 5 * samples]
    deltas = deltas_ref[...]
    first = lax.broadcasted_iota(jnp.int32, (samples, samples), 0)
    second = lax.broadcasted_iota(jnp.int32, (samples, samples), 1)
    earlier = jnp.where(second < first, 1.0, 0.0)
    later = jnp.where(second > first, 1.0, 0.0)
    tail = jnp.exp(-jnp.abs(raw[0]))
    softplus = jnp.maximum(raw[0], 0.0) + jnp.log1p(tail)
    optical = routed * softplus * deltas
    before = nn(earlier, optical, HIGH)
    total = jnp.sum(optical, axis=0, keepdims=True)
    through = jnp.exp(-before)
    kept = jnp.exp(-optical)
    weight = through * (1.0 - kept)
    leaving = jnp.exp(-total)
    back_slope = jnp.zeros_like(total)
    weight_slope = jnp.zeros_like(weight)
    slope_parts = []
    for k in range(3):
        color = jax.nn.sigmoid(raw[k + 1])
        pixel = jnp.sum(weight * color, axis=0, keepdims=True) + leaving * back_ref[k : k + 1]
        pixel_slope = loss_scale * (pixel - target_ref[k : k + 1])
        back_slope = back_slope + pixel_slope * back_ref[k : k + 1]
        weight_slope = weight_slope + pixel_slope * color
        slope_parts.append((weight * pixel_slope * (color * (1.0 - color))).astype(BF16))
    after = nn(later, weight_slope * weight, HIGH)
    optical_slope = weight_slope * through * kept - after - leaving * back_slope
    density_slope = optical_slope * deltas * routed * jax.nn.sigmoid(raw[0])
    stacked = jnp.concatenate([density_slope.astype(BF16)] + slope_parts, axis=0)
    sums_ref[...] = jnp.zeros_like(sums_ref)

    def spread_slopes(step, carry):
        here = pl.ds(pl.multiple_of(step * chunk, 128), chunk)
        ray_hot = hot_bf16(one_hot(ray_ref[:, here], rays))
        sam_hot = one_hot(sam_ref[:, here], samples)
        first_slot, slot_id = slot_places(step, chunk)
        cell_hot = (slot_id >= first_slot) & (slot_id < first_slot + capacity)
        picked = nn(stacked, ray_hot)
        spread = []
        for k in range(4):
            part = picked[k * samples : (k + 1) * samples]
            column = jnp.sum(jnp.where(sam_hot, part, 0.0), axis=0, keepdims=True)
            slope_ref[k : k + 1, here] = column
            if k:
                spread.append(jnp.where(cell_hot, column, 0.0).astype(BF16))
        sums_ref[...] += nt(jnp.concatenate(spread, axis=0), ray_hot)
        return carry

    in_pairs(steps, spread_slopes)
    for n in range(owners):
        slope_send[n] = slope_ref[:, n * per_owner : (n + 1) * per_owner]
    slope_args = (
        me,
        owners,
        lambda n: slope_send.at[n],
        slope_land,
        send_sems.at[3],
        recv_sems.at[3],
    )
    start_all(*slope_args)
    slope_land[me] = slope_send[me]
    sums = sums_ref[...]
    partial_ref[...] = nt(sums, app_ref[...], HIGH)
    terms = tn(heads_ref[...], sums, HIGH)

    def place_terms(n, carry):
        term_send[n, :app_width, :rays] = terms
        for k in range(3):
            term_send[
                n, app_width + k * cell_dev : app_width + (k + 1) * cell_dev, :app_width
            ] = partial_ref[pl.ds(k * cells + n * cell_dev, cell_dev), :]
        return carry

    lax.fori_loop(0, owners, place_terms, 0)
    term_args = (
        me,
        owners,
        lambda n: term_send.at[n],
        term_land,
        send_sems.at[4],
        recv_sems.at[4],
    )
    wait_all(*slope_args)
    start_all(*term_args)
    term_land[me] = term_send[me]
    for j in range(cell_dev):
        cellslope_ref[j] = jnp.concatenate(
            [slope_land[n][:, j * capacity : (j + 1) * capacity] for n in range(owners)], axis=1
        )

    def backward(step, carry):
        j = step // blocks
        here = pl.ds(pl.multiple_of((step % blocks) * lanes, 128), lanes)
        slopes = cellslope_ref[j, :, here].astype(BF16)
        ones = jnp.ones((8, lanes), BF16)
        gh_ref[j] += nt(slopes, act2_ref[j, :, here])
        delta = (tn(head_ref[j], slopes) * d2_ref[j, :, here]).astype(BF16)
        gw2_ref[j] += nt(act1_ref[j, :, here], delta)
        gb2_ref[pl.ds(j, 1), :] += nt(ones, delta)[0:1]
        delta = (nn(w2_ref[j], delta) * d1_ref[j, :, here]).astype(BF16)
        gw1_ref[j] += nt(enc_ref[j, :, here], delta)
        gb1_ref[pl.ds(j, 1), :] += nt(ones, delta)[0:1]
        return carry

    in_pairs(cell_dev * blocks, backward)

    wait_all(*term_args)
    total = term_land[0]
    for n in range(1, owners):
        total = total + term_land[n]
    for j in range(cell_dev):
        for k in range(3):
            row = app_width + k * cell_dev + j
            ga_ref[j, k : k + 1, :] = total[row : row + 1, :app_width]
    terms = jnp.concatenate([term_land[n][:app_width, :rays] for n in range(owners)], axis=1)
    term_parts = jnp.concatenate(split3(terms), axis=0)
    if not kept_hot:
        all_codes = codes_of_all()
    for first_code in range(0, codes_total, block):
        if kept_hot:
            hot = hot_ref[first_code : first_code + block, :]
        else:
            hot = hot_bf16(one_hot(all_codes - first_code, block))
        sums = nt(term_parts, hot)
        gt_ref[:, first_code : first_code + block] = (
            sums[2 * app_width :] + sums[app_width : 2 * app_width]
        ) + sums[:app_width]


def local(
    positions,
    deltas,
    background,
    target,
    ray_codes,
    frequencies,
    w_first,
    b_first,
    w_second,
    b_second,
    head_out,
    head_app,
    app_table,
    dispatch,
    counts,
):
    owners = lax.axis_size("cell")
    lists, capacity = dispatch.shape
    cell_dev, encoding, width = w_first.shape
    rows_local = positions.shape[1]
    rays = ray_codes.shape[0]
    samples = rows_local // rays
    app_width, codes_total = app_table.shape
    slots_cell = owners * capacity

    listed = dispatch.reshape(1, rows_local)
    slot_ray = listed // samples
    slot_sam = listed - slot_ray * samples
    pos_grid = jnp.transpose(positions.reshape(3, rays, samples), (0, 2, 1))
    delta_grid = deltas.reshape(rays, samples).T

    per_owner = cell_dev * capacity
    side = max(rays, app_width)
    extra = jnp.transpose(head_app.astype(F32), (1, 0, 2)).reshape(3 * cell_dev, app_width)
    extra = jnp.concatenate(
        [
            jnp.pad(extra, ((0, 0), (0, side - app_width))),
            jnp.pad(ray_codes.astype(F32)[None, :], ((0, 0), (0, side - rays))),
        ],
        axis=0,
    )
    term_rows = app_width + 3 * cell_dev
    hot_rows = codes_total if owners * rays <= 2048 else 16
    in_vmem = pl.BlockSpec(memory_space=pltpu.VMEM)
    outs = (
        jax.ShapeDtypeStruct((cell_dev, encoding, width), F32),
        jax.ShapeDtypeStruct((cell_dev, width), F32),
        jax.ShapeDtypeStruct((cell_dev, width, width), F32),
        jax.ShapeDtypeStruct((cell_dev, width), F32),
        jax.ShapeDtypeStruct((cell_dev, 4, width), F32),
        jax.ShapeDtypeStruct((cell_dev, 3, app_width), F32),
        jax.ShapeDtypeStruct((app_width, codes_total), F32),
    )
    (
        grad_w_first,
        grad_b_first,
        grad_w_second,
        grad_b_second,
        grad_head_out,
        grad_head_app,
        grad_table,
    ) = pl.pallas_call(
        functools.partial(whole_kernel, owners, capacity),
        out_shape=outs,
        in_specs=[in_vmem] * 16,
        out_specs=(in_vmem,) * 7,
        scratch_shapes=[
            pltpu.VMEM((owners,) + extra.shape, F32),
            pltpu.VMEM((owners, 3, per_owner), F32),
            pltpu.VMEM((owners, 3, per_owner), F32),
            pltpu.VMEM((owners, 4, per_owner), F32),
            pltpu.VMEM((owners, 4, per_owner), F32),
            pltpu.VMEM((owners, 4, per_owner), F32),
            pltpu.VMEM((owners, 4, per_owner), F32),
            pltpu.VMEM((owners, term_rows, side), F32),
            pltpu.VMEM((owners, term_rows, side), F32),
            pltpu.VMEM((3, rows_local), F32),
            pltpu.VMEM((cell_dev, 3, slots_cell), F32),
            pltpu.VMEM((cell_dev, encoding, slots_cell), BF16),
            pltpu.VMEM((cell_dev, width, slots_cell), BF16),
            pltpu.VMEM((cell_dev, width, slots_cell), BF16),
            pltpu.VMEM((cell_dev, width, slots_cell), F32),
            pltpu.VMEM((cell_dev, width, slots_cell), F32),
            pltpu.VMEM((cell_dev, 4, slots_cell), F32),
            pltpu.VMEM((cell_dev, 4, slots_cell), F32),
            pltpu.VMEM((4, rows_local), F32),
            pltpu.VMEM((4, rows_local), F32),
            pltpu.VMEM((3 * lists, app_width), F32),
            pltpu.VMEM((app_width, rays), F32),
            pltpu.VMEM((3 * lists, app_width), F32),
            pltpu.VMEM((3 * lists, rays), F32),
            pltpu.VMEM((5 * samples, rays), F32),
            pltpu.VMEM((3 * lists, rays), F32),
            pltpu.VMEM((frequencies.shape[1], 3), F32),
            pltpu.VMEM((cell_dev, width, 1), F32),
            pltpu.VMEM((cell_dev, width, 1), F32),
            pltpu.VMEM((hot_rows, owners * rays), BF16),
            pltpu.SemaphoreType.DMA((5, owners)),
            pltpu.SemaphoreType.DMA((5, owners)),
        ],
        compiler_params=pltpu.CompilerParams(
            vmem_limit_bytes=56 * 1024 * 1024, collective_id=0, has_side_effects=True
        ),
        name="whole",
    )(
        slot_ray,
        slot_sam,
        counts.reshape(1, lists),
        pos_grid,
        ray_codes.reshape(1, rays),
        app_table,
        extra,
        frequencies,
        w_first,
        b_first,
        w_second,
        b_second,
        head_out,
        delta_grid,
        background,
        target,
    )
    return (
        grad_w_first,
        grad_b_first,
        grad_w_second,
        grad_b_second,
        grad_head_out,
        grad_head_app,
        grad_table,
    )


def solution(mesh):
    placed = (
        P(None, ("groups", "cell")),
        P(("groups", "cell")),
        P(None, ("groups", "cell")),
        P(None, ("groups", "cell")),
        P(("groups", "cell")),
        P(),
        P("cell", None, None),
        P("cell", None),
        P("cell", None, None),
        P("cell", None),
        P("cell", None, None),
        P("cell", None, None),
        P(),
        P(("groups", "cell"), None),
        P(("groups", "cell")),
    )
    return jax.shard_map(
        local,
        mesh=mesh,
        in_specs=placed,
        out_specs=(
            P(("groups", "cell"), None, None),
            P(("groups", "cell"), None),
            P(("groups", "cell"), None, None),
            P(("groups", "cell"), None),
            P(("groups", "cell"), None, None),
            P(("groups", "cell"), None, None),
            P("groups", None),
        ),
        check_vma=False,
    )
```
